128 devices in a mesh: tok: 4 (over y_lo, core), tp: 32 (over x, z, y_hi).
Axes of the slice: x: 4, y: 4 (y_hi: 2, y_lo: 2; y = y_hi * 2 + y_lo), z: 4, core: 2. Of those that a mesh axis runs over, the one named last changes fastest.
Arguments:
- residual: bfloat16 [1024, 16384], P('tok', 'tp')
- norm_gain: float32 [16384], replicated, may hold values from 0.5 to 1.5
- weight: bfloat16 [30720, 16384], P(('tok', 'tp')), may hold values from -6 to 6
- scale_codes: int32 [30720, 2], P(('tok', 'tp')), may hold values from 0 to 7
- zero_points: int32 [30720, 2], P(('tok', 'tp')), may hold values from 4 to 11
- panels: bfloat16 [256, 16384], P(None, ('tok', 'tp')), as said below
Outputs:
- gram: float32 [16384, 16384], P('tok', 'tp')
- quantized: bfloat16 [30720, 16384], P('tok', 'tp')
The draws below stay inside these ranges and needn't reach their ends.
Inputs may be any that keep to these rules, and one draw needn't show every extreme that they name: Row j of panels is row j of an upper-triangular factor: entries left of column j are zero and panels[j, j] lies in [0.5, 1.5].
All inputs are finite; a program needn't handle non-finite values.
Results may differ from the reference program's by a relative error of at most 0.0085.
Values may be sent and summed in bfloat16 or wider, within the bound.
No kernel may reach another device: no remote copies, remote signals or barrier semaphores. Data moves between devices by JAX's collectives and lax.ppermute only.
A program may use at most 192 MiB of HBM per device.

```python
import math
import jax
import jax.numpy as jnp
from jax import lax

D = 16384
FF = 30720
TOK_DEV = 256
BLOCK = 128
BLOCKS = 2
TOKENS = 1024
N_TOK = 4


def draw_residual(key, part):
    key_cols, key_rows, key_base = jax.random.split(key, 3)
    place = jnp.arange(D, dtype=jnp.float32) / D
    col_scale = jnp.exp(math.log(10.0) * place + jax.random.uniform(key_cols, (D,), minval=-0.5, maxval=0.5))
    row_scale = jnp.exp(jax.random.uniform(key_rows, (TOKENS, 1), minval=0.0, maxval=math.log(10.0)))
    base = jax.random.normal(key_base, (TOKENS, D))
    return (base * col_scale[None, :] * row_scale).astype(jnp.bfloat16)


def draw_panels(key, part):
    key_off, key_diag = jax.random.split(key)
    row_ids = jnp.arange(BLOCKS * BLOCK, dtype=jnp.int32)[:, None]
    col_ids = jnp.arange(D, dtype=jnp.int32)[None, :]
    spread = 0.12 * jax.random.normal(key_off, (BLOCKS * BLOCK, D))
    pivots = jax.random.uniform(key_diag, (BLOCKS * BLOCK, 1), minval=0.5, maxval=1.5)
    values = jnp.where(col_ids > row_ids, spread, jnp.where(col_ids == row_ids, pivots, 0.0))
    return values.astype(jnp.bfloat16)


def set_ends(entries, key, smallest, top_value):
    extent = entries.shape
    spot = [jax.random.randint(jax.random.fold_in(key, axis), (), 0, extent[axis]) for axis in range(len(extent))]
    entries = entries.at[tuple(spot)].set(smallest)
    longest = extent.index(max(extent))
    spot[longest] = (spot[longest] + 1) % extent[longest]
    return entries.at[tuple(spot)].set(top_value)


def block_levels(own_key, dims, cuts, low, largest):
    gain, own = 1.0, jax.random.fold_in(own_key, 6)
    for axis_at, shards_of in cuts:
        draws = jnp.exp(jax.random.uniform(jax.random.fold_in(own, axis_at), (shards_of,), jnp.float32, low / len(cuts), largest / len(cuts)))
        gain = gain * jnp.repeat(draws, dims[axis_at] // shards_of).reshape([-1 if axis == axis_at else 1 for axis in range(len(dims))])
    return gain


def scatter_about(rng, extent, deviation, bound, cuts=(), kind=jnp.bfloat16):
    drawn = deviation * jax.random.normal(rng, extent, jnp.float32)
    if cuts:
        drawn = drawn * block_levels(rng, extent, cuts, -0.22, 0.18)
    return jnp.clip(drawn, -bound, bound).astype(kind)


def setup_inputs(seed: int = 0) -> dict:
    key_of = jax.random.split(jax.random.key(seed), 7)
    return {
        "residual": draw_residual(jax.random.fold_in(key_of[6], 71), 0),
        "norm_gain": jnp.clip(1.0 + 0.1 * jax.random.normal(key_of[1], (D,), jnp.float32), 0.5, 1.5),
        "weight": scatter_about(key_of[2], (FF, D), 1.0, 6.0, ((0, 128),)),
        "scale_codes": set_ends(jax.random.randint(key_of[3], (FF, BLOCKS), 0, 8), jax.random.fold_in(key_of[3], 1), 0, 7).astype(jnp.int32),
        "zero_points": set_ends(jax.random.randint(key_of[4], (FF, BLOCKS), 4, 12), jax.random.fold_in(key_of[4], 1), 4, 11).astype(jnp.int32),
        "panels": draw_panels(jax.random.fold_in(key_of[6], 71), 0),
    }


EPS = 1e-05
SOFTNESS = 0.9
FULL_TURN = 2.0 * math.pi

def dequantize(column, scale_row, zero_row):
    shifted = column / scale_row + zero_row
    softened = shifted - SOFTNESS * jnp.sin(FULL_TURN * shifted) / FULL_TURN
    return scale_row * (jnp.clip(softened, 0.0, 15.0) - zero_row)

def reference(residual, norm_gain, weight, scale_codes, zero_points, panels):
    resid_f = residual.astype(jnp.float32)
    mean_square = lax.optimization_barrier(jnp.mean(resid_f * resid_f, axis=1, keepdims=True))
    normed = (resid_f * lax.rsqrt(mean_square + EPS) * norm_gain[None, :]).astype(jnp.bfloat16)
    groups = normed.astype(jnp.float32).reshape(N_TOK, TOK_DEV, D)
    col_width = D // 16

    def gram_block(block_id):
        cols_first = block_id * col_width
        running = jnp.zeros((D, col_width), jnp.float32)
        for g in range(N_TOK):
            group_rows = groups[g]
            right_cols = lax.dynamic_slice_in_dim(group_rows, cols_first, col_width, 1)
            group_term = lax.dot_general(group_rows, right_cols, (((0,), (0,)), ((), ())), preferred_element_type=jnp.float32)
            rounded = lax.optimization_barrier(group_term.astype(jnp.bfloat16))
            running = running + rounded.astype(jnp.float32)
        return running / TOKENS
    blocks_out = lax.map(gram_block, jnp.arange(16, dtype=jnp.int32))
    gram = jnp.transpose(blocks_out, (1, 0, 2)).reshape(D, D)
    column = jnp.arange(D, dtype=jnp.int32)
    lane_ids = jnp.arange(BLOCK, dtype=jnp.int32)

    def quantize_rows(inputs):
        weight_rows, codes, zeros_in = inputs
        working = weight_rows.astype(jnp.float32)
        for k in range(BLOCKS):
            block_start = k * BLOCK
            scale_row = jnp.exp2(codes[:, k].astype(jnp.float32) * 0.5 - 3.0)
            zero_row = zeros_in[:, k].astype(jnp.float32)
            panel_rows = panels[block_start:block_start + BLOCK].astype(jnp.float32)
            diagonal = panel_rows[:, block_start:block_start + BLOCK]

            def column_step(block_cols, j):
                column_now = lax.dynamic_index_in_dim(block_cols, j, 1, keepdims=False)
                pivot_row = lax.dynamic_index_in_dim(diagonal, j, 0, keepdims=False)
                pivot = jnp.sum(jnp.where(lane_ids == j, pivot_row, 0.0))
                restored = dequantize(column_now, scale_row, zero_row)
                error_now = (column_now - restored) / pivot
                block_cols = block_cols - error_now[:, None] * jnp.where(lane_ids > j, pivot_row, 0.0)[None, :]
                block_cols = jnp.where((lane_ids == j)[None, :], restored[:, None], block_cols)
                return (block_cols, error_now)
            block_cols, errors = lax.scan(column_step, working[:, block_start:block_start + BLOCK], lane_ids)
            correction = jnp.dot(errors.T, panel_rows, precision=lax.Precision.HIGHEST)
            working = jnp.where((column >= block_start + BLOCK)[None, :], working - correction, working)
            working = working.at[:, block_start:block_start + BLOCK].set(block_cols)
        return working.astype(jnp.bfloat16)
    row_blocks = max(1, FF // 2048)
    stacked = lax.map(quantize_rows, (weight.reshape(row_blocks, FF // row_blocks, D), scale_codes.reshape(row_blocks, FF // row_blocks, BLOCKS), zero_points.reshape(row_blocks, FF // row_blocks, BLOCKS)))
    quantized = stacked.reshape(FF, D)
    return (gram, quantized)
```

```python
import functools
import math

import jax
import jax.numpy as jnp
from jax import lax
from jax.experimental import pallas as pl
from jax.experimental.pallas import tpu as pltpu
from jax.sharding import PartitionSpec as P

BLOCK = 128
BLOCKS = 2
COLS = BLOCK * BLOCKS
SUB = 8

EPS = 1e-05
SOFTNESS = 0.9
ALL = ("tok", "tp")

SINE = tuple(
    c * SOFTNESS / (2.0 * math.pi)
    for c in (
        6.283182818496983,
        -41.341421393740156,
        81.59618374823393,
        -76.58009925759313,
        41.20538928368347,
        -12.271253496065944,
    )
)


def tp_index(x, z, h):
    return x * 8 + z * 2 + h


def index(t, x, z, h):
    return t * 32 + tp_index(x, z, h)


PLACES = [(t, x, z, h) for t in range(4) for x in range(4) for z in range(4) for h in range(2)]


def moves(fn):
    return [(index(*a), index(*fn(*a))) for a in PLACES]


def split3(v):
    hi = v.astype(jnp.bfloat16).astype(jnp.float32)
    rest = v - hi
    mid = rest.astype(jnp.bfloat16).astype(jnp.float32)
    return hi, mid, rest - mid


def contract_rows(a, b):
    return lax.dot_general(a, b, (((0,), (0,)), ((), ())), preferred_element_type=jnp.float32)


def errors_kernel(w_ref, codes_ref, zeros_ref, p_ref, e_ref, work, diag, panel, errs):
    rows = w_ref.shape[0]
    lanes = work.shape[1]
    w = w_ref[...].astype(jnp.float32)
    w = jnp.concatenate([w, jnp.zeros((lanes - rows, COLS), jnp.float32)], axis=0)
    work[...] = w.T
    panel[...] = p_ref[...].astype(jnp.float32)
    across = panel[...].T
    row_id = lax.broadcasted_iota(jnp.int32, (COLS, COLS), 0)
    col_id = lax.broadcasted_iota(jnp.int32, (COLS, COLS), 1)
    pivots = jnp.sum(jnp.where(row_id == col_id, across, 0.0), axis=1, keepdims=True)
    diag[:, SUB : SUB + 1] = 1.0 / pivots
    for g in range(COLS // SUB):
        diag[g * SUB : (g + 1) * SUB, :SUB] = across[g * SUB : (g + 1) * SUB, g * SUB : (g + 1) * SUB]
    sub_id = lax.broadcasted_iota(jnp.int32, (SUB, lanes), 0)
    for k in range(BLOCKS):
        first = k * BLOCK
        half = codes_ref[k : k + 1, :] * 0.5 - 3.0
        scale = jnp.broadcast_to(jnp.exp2(half), (SUB, lanes))
        inverse = jnp.broadcast_to(jnp.exp2(-half), (SUB, lanes))
        zero = jnp.broadcast_to(zeros_ref[k : k + 1, :], (SUB, lanes))

        def group(g, carry):
            base = pl.multiple_of(first + g * SUB, SUB)
            now = work[pl.ds(base, SUB), :]
            local = diag[pl.ds(base, SUB), :]
            inv_pivot = jnp.broadcast_to(local[:, SUB : SUB + 1], (SUB, lanes))
            found = jnp.zeros((SUB, lanes), jnp.float32)
            for i in range(SUB):
                u = now * inverse + zero
                r = u - jnp.round(u)
                r2 = r * r
                r4 = r2 * r2
                wave = (SINE[0] + SINE[1] * r2) + r4 * (
                    (SINE[2] + SINE[3] * r2) + r4 * (SINE[4] + SINE[5] * r2)
                )
                soft = jnp.clip(u - wave * r, 0.0, 15.0)
                error = (now - scale * (soft - zero)) * inv_pivot
                error = jnp.broadcast_to(error[i : i + 1, :], (SUB, lanes))
                now = now - jnp.broadcast_to(local[:, i : i + 1], (SUB, lanes)) * error
                found = jnp.where(sub_id == i, error, found)
            errs[pl.ds(base, SUB), :] = found
            p_rows = panel[pl.ds(base, SUB), first : first + BLOCK]
            p_rows = jnp.concatenate([p_rows] * 3, axis=0).astype(jnp.bfloat16)
            e_rows = jnp.concatenate(split3(found), axis=0).astype(jnp.bfloat16)
            work[first : first + BLOCK, :] -= contract_rows(p_rows, e_rows)
            return carry

        lax.fori_loop(0, BLOCK // SUB, group, 0)
        if k + 1 < BLOCKS:
            p_rows = panel[first : first + BLOCK, first + BLOCK :].astype(jnp.bfloat16)
            spill = 0.0
            for part in split3(errs[first : first + BLOCK, :]):
                spill = spill + contract_rows(p_rows, part.astype(jnp.bfloat16))
            work[first + BLOCK :, :] -= spill
    e_ref[...] = errs[...].T[:rows].astype(jnp.bfloat16)


def block_errors(weight, codes, zeros, first_panel):
    rows = weight.shape[0]
    lanes = -(-rows // 128) * 128
    return pl.pallas_call(
        errors_kernel,
        grid=(1,),
        out_shape=jax.ShapeDtypeStruct((rows, COLS), jnp.bfloat16),
        in_specs=[
            pl.BlockSpec((rows, COLS), lambda i: (0, 0)),
            pl.BlockSpec((BLOCKS, lanes), lambda i: (0, 0)),
            pl.BlockSpec((BLOCKS, lanes), lambda i: (0, 0)),
            pl.BlockSpec((COLS, COLS), lambda i: (0, 0)),
        ],
        out_specs=pl.BlockSpec((rows, COLS), lambda i: (0, 0)),
        scratch_shapes=[
            pltpu.VMEM((COLS, lanes), jnp.float32),
            pltpu.VMEM((COLS, 128), jnp.float32),
            pltpu.VMEM((COLS, COLS), jnp.float32),
            pltpu.VMEM((COLS, lanes), jnp.float32),
        ],
        compiler_params=pltpu.CompilerParams(vmem_limit_bytes=16 * 2**20),
        cost_estimate=pl.CostEstimate(flops=10**7, bytes_accessed=10**6, transcendentals=0),
        name="errors",
    )(weight, codes, zeros, first_panel)


def gram_kernel(total, rows_ref, own_ref, inv_ref, gain_rows_ref, gain_own_ref, out_ref, own):
    @pl.when(pl.program_id(0) == 0)
    def _():
        for g in range(own_ref.shape[0]):
            v = own_ref[g].astype(jnp.float32) * inv_ref[g] * gain_own_ref[...]
            own[g] = v.astype(jnp.bfloat16)

    acc = 0.0
    for g in range(own_ref.shape[0]):
        v = rows_ref[g, 0].astype(jnp.float32) * inv_ref[g] * gain_rows_ref[0]
        acc = acc + contract_rows(v.astype(jnp.bfloat16), own[g])
    out_ref[...] = acc * (1.0 / total)


def mean_outer(quarter, own, inv_norm, gain_rows, gain_own):
    groups, pieces, toks, feats = quarter.shape
    return pl.pallas_call(
        functools.partial(gram_kernel, groups * toks),
        grid=(pieces,),
        out_shape=jax.ShapeDtypeStruct((pieces * feats, feats), jnp.float32),
        in_specs=[
            pl.BlockSpec((groups, 1, toks, feats), lambda i: (0, i, 0, 0)),
            pl.BlockSpec((groups, toks, feats), lambda i: (0, 0, 0)),
            pl.BlockSpec((groups, toks, 1), lambda i: (0, 0, 0)),
            pl.BlockSpec((1, 1, feats), lambda i: (i, 0, 0)),
            pl.BlockSpec((1, feats), lambda i: (0, 0)),
        ],
        out_specs=pl.BlockSpec((feats, feats), lambda i: (i, 0)),
        scratch_shapes=[pltpu.VMEM((groups, toks, feats), jnp.bfloat16)],
        compiler_params=pltpu.CompilerParams(vmem_limit_bytes=32 * 2**20),
        cost_estimate=pl.CostEstimate(
            flops=2 * groups * toks * pieces * feats * feats,
            bytes_accessed=20 * 2**20,
            transcendentals=0,
        ),
        name="mean_outer",
    )(quarter, own, inv_norm, gain_rows.reshape(pieces, 1, feats), gain_own.reshape(1, feats))


def corrected_kernel(w_ref, e_ref, p_ref, out_ref):
    correction = jnp.dot(e_ref[...], p_ref[...], preferred_element_type=jnp.float32)
    out_ref[...] = (w_ref[...].astype(jnp.float32) - correction).astype(jnp.bfloat16)


def corrected(moved, errors, panel):
    rows, feats = moved.shape
    step = rows // 16
    return pl.pallas_call(
        corrected_kernel,
        grid=(rows // step,),
        out_shape=jax.ShapeDtypeStruct((rows, feats), jnp.bfloat16),
        in_specs=[
            pl.BlockSpec((step, feats), lambda i: (i, 0)),
            pl.BlockSpec((step, COLS), lambda i: (i, 0)),
            pl.BlockSpec((COLS, feats), lambda i: (0, 0)),
        ],
        out_specs=pl.BlockSpec((step, feats), lambda i: (i, 0)),
        compiler_params=pltpu.CompilerParams(vmem_limit_bytes=16 * 2**20),
        cost_estimate=pl.CostEstimate(
            flops=2 * rows * feats * COLS, bytes_accessed=20 * 2**20, transcendentals=0
        ),
        name="corrected",
    )(moved, errors, panel)


def first_columns(panels, t, p):
    nothing = jnp.zeros_like(panels)
    held = jnp.concatenate(
        [
            jnp.where((t == 0) & (p == 0), panels, nothing),
            jnp.where((t == 0) & (p == 1), panels, nothing),
        ],
        axis=1,
    )

    def step(held, perms):
        for got in [lax.ppermute(held, ALL, perm) for perm in perms]:
            held = held + got
        return held

    four = range(4)
    held = step(held, [[(index(0, 0, 0, h), index(0, 0, 0, 1 - h)) for h in range(2)]])
    held = step(
        held,
        [[(index(0, 0, 0, h), index(0, x, 0, h)) for h in range(2)] for x in (1, 2, 3)],
    )
    held = step(
        held,
        [
            [(index(0, x, 0, h), index(0, x, z, h)) for x in four for h in range(2)]
            for z in (1, 2, 3)
        ],
    )
    return step(
        held,
        [
            [(index(0, x, z, h), index(t, x, z, h)) for x in four for z in four for h in range(2)]
            for t in (1, 2, 3)
        ],
    )


def own_columns(panels, t):
    def target(k):
        def to(tt, x, z, h):
            i = (z % 2) * 2 + h
            return (i ^ k, tt, x, z // 2)

        return to

    got = jnp.stack([lax.ppermute(panels, ALL, moves(target(k))) for k in range(4)])
    order = [lax.dynamic_index_in_dim(got, t ^ i, 0, keepdims=False) for i in range(4)]
    return jnp.concatenate(order, axis=1)


def on_device(residual, norm_gain, weight, scale_codes, zero_points, panels):
    toks, feats = residual.shape
    rows, feat_total = weight.shape
    t = lax.axis_index("tok")
    p = lax.axis_index("tp")
    shards = lax.axis_size("tp")
    groups = lax.axis_size("tok")
    pieces = shards // groups

    swapped = lax.ppermute(residual, ALL, moves(lambda tt, x, z, h: (x, tt, z, h)))
    quarter = lax.all_gather(swapped, "tp").reshape(groups, pieces, toks, feats)
    own = lax.all_gather(residual, "tok")

    first_panel = first_columns(panels, t, p)
    pad = -(-rows // 128) * 128 - rows
    codes = jnp.pad(scale_codes.astype(jnp.float32).T, ((0, 0), (0, pad)))
    zeros = jnp.pad(zero_points.astype(jnp.float32).T, ((0, 0), (0, pad)))
    errors = block_errors(weight[:, :COLS], codes, zeros, first_panel)
    errors_all = lax.all_gather(errors, "tp", axis=0, tiled=True)
    own_panel = own_columns(panels, t)

    moved = lax.all_to_all(weight, "tp", split_axis=1, concat_axis=0, tiled=True)

    squares = quarter.astype(jnp.float32)
    sums = jnp.sum(squares * squares, axis=(1, 3))
    sums = sums + lax.ppermute(sums, ALL, moves(lambda tt, x, z, h: (tt ^ 1, x, z, h)))
    sums = sums + lax.ppermute(sums, ALL, moves(lambda tt, x, z, h: (tt ^ 2, x, z, h)))
    inv_norm = lax.rsqrt(sums / feat_total + EPS)[:, :, None]
    quarter_feats = feat_total // groups
    gain_rows = lax.dynamic_slice_in_dim(norm_gain, t * quarter_feats, quarter_feats, 0)
    gain_own = lax.dynamic_slice_in_dim(norm_gain, p * feats, feats, 0)
    gram = mean_outer(quarter, own, inv_norm, gain_rows, gain_own)

    return (gram, corrected(moved, errors_all, own_panel))


def solution(mesh):
    in_specs = (
        P("tok", "tp"),
        P(),
        P(("tok", "tp"), None),
        P(("tok", "tp"), None),
        P(("tok", "tp"), None),
        P(None, ("tok", "tp")),
    )
    out_specs = (P("tok", "tp"), P("tok", "tp"))
    return jax.shard_map(
        on_device, mesh=mesh, in_specs=in_specs, out_specs=out_specs, check_vma=False
    )
```

```python
import functools
import math

import jax
import jax.numpy as jnp
from jax import lax
from jax.experimental import pallas as pl
from jax.experimental.pallas import tpu as pltpu
from jax.sharding import PartitionSpec as P

BLOCK = 128
BLOCKS = 2
COLS = BLOCK * BLOCKS
SUB = 8

EPS = 1e-05
SOFTNESS = 0.9
ALL = ("tok", "tp")

SINE = tuple(
    c * SOFTNESS / (2.0 * math.pi)
    for c in (
        6.283182818496983,
        -41.341421393740156,
        81.59618374823393,
        -76.58009925759313,
        41.20538928368347,
        -12.271253496065944,
    )
)


def tp_index(x, z, h):
    return x * 8 + z * 2 + h


def index(t, x, z, h):
    return t * 32 + tp_index(x, z, h)


PLACES = [(t, x, z, h) for t in range(4) for x in range(4) for z in range(4) for h in range(2)]


def moves(fn):
    return [(index(*a), index(*fn(*a))) for a in PLACES]


def split3(v):
    hi = v.astype(jnp.bfloat16).astype(jnp.float32)
    rest = v - hi
    mid = rest.astype(jnp.bfloat16).astype(jnp.float32)
    return hi, mid, rest - mid


def contract_rows(a, b):
    return lax.dot_general(a, b, (((0,), (0,)), ((), ())), preferred_element_type=jnp.float32)


def errors_kernel(w_ref, codes_ref, zeros_ref, p_ref, e_ref, work, diag, panel, errs):
    rows = w_ref.shape[0]
    lanes = work.shape[1]
    w = w_ref[...].astype(jnp.float32)
    w = jnp.concatenate([w, jnp.zeros((lanes - rows, COLS), jnp.float32)], axis=0)
    work[...] = w.T
    panel[...] = p_ref[...].astype(jnp.float32)
    across = panel[...].T
    row_id = lax.broadcasted_iota(jnp.int32, (COLS, COLS), 0)
    col_id = lax.broadcasted_iota(jnp.int32, (COLS, COLS), 1)
    pivots = jnp.sum(jnp.where(row_id == col_id, across, 0.0), axis=1, keepdims=True)
    diag[:, SUB : SUB + 1] = 1.0 / pivots
    for g in range(COLS // SUB):
        diag[g * SUB : (g + 1) * SUB, :SUB] = across[g * SUB : (g + 1) * SUB, g * SUB : (g + 1) * SUB]
    sub_id = lax.broadcasted_iota(jnp.int32, (SUB, lanes), 0)
    for k in range(BLOCKS):
        first = k * BLOCK
        half = codes_ref[k : k + 1, :] * 0.5 - 3.0
        scale = jnp.broadcast_to(jnp.exp2(half), (SUB, lanes))
        inverse = jnp.broadcast_to(jnp.exp2(-half), (SUB, lanes))
        zero = jnp.broadcast_to(zeros_ref[k : k + 1, :], (SUB, lanes))

        def group(g, carry):
            base = pl.multiple_of(first + g * SUB, SUB)
            now = work[pl.ds(base, SUB), :]
            local = diag[pl.ds(base, SUB), :]
            inv_pivot = jnp.broadcast_to(local[:, SUB : SUB + 1], (SUB, lanes))
            found = jnp.zeros((SUB, lanes), jnp.float32)
            for i in range(SUB):
                u = now * inverse + zero
                r = u - jnp.round(u)
                r2 = r * r
                r4 = r2 * r2
                wave = (SINE[0] + SINE[1] * r2) + r4 * (
                    (SINE[2] + SINE[3] * r2) + r4 * (SINE[4] + SINE[5] * r2)
                )
                soft = jnp.clip(u - wave * r, 0.0, 15.0)
                error = (now - scale * (soft - zero)) * inv_pivot
                error = jnp.broadcast_to(error[i : i + 1, :], (SUB, lanes))
                now = now - jnp.broadcast_to(local[:, i : i + 1], (SUB, lanes)) * error
                found = jnp.where(sub_id == i, error, found)
            errs[pl.ds(base, SUB), :] = found
            p_rows = panel[pl.ds(base, SUB), first : first + BLOCK]
            p_rows = jnp.concatenate([p_rows] * 3, axis=0).astype(jnp.bfloat16)
            e_rows = jnp.concatenate(split3(found), axis=0).astype(jnp.bfloat16)
            work[first : first + BLOCK, :] -= contract_rows(p_rows, e_rows)
            return carry

        lax.fori_loop(0, BLOCK // SUB, group, 0)
        if k + 1 < BLOCKS:
            p_rows = panel[first : first + BLOCK, first + BLOCK :].astype(jnp.bfloat16)
            spill = 0.0
            for part in split3(errs[first : first + BLOCK, :]):
                spill = spill + contract_rows(p_rows, part.astype(jnp.bfloat16))
            work[first + BLOCK :, :] -= spill
    e_ref[...] = errs[...].T[:rows].astype(jnp.bfloat16)


def block_errors(weight, codes, zeros, first_panel):
    rows = weight.shape[0]
    lanes = -(-rows // 128) * 128
    return pl.pallas_call(
        errors_kernel,
        grid=(1,),
        out_shape=jax.ShapeDtypeStruct((rows, COLS), jnp.bfloat16),
        in_specs=[
            pl.BlockSpec((rows, COLS), lambda i: (0, 0)),
            pl.BlockSpec((BLOCKS, lanes), lambda i: (0, 0)),
            pl.BlockSpec((BLOCKS, lanes), lambda i: (0, 0)),
            pl.BlockSpec((COLS, COLS), lambda i: (0, 0)),
        ],
        out_specs=pl.BlockSpec((rows, COLS), lambda i: (0, 0)),
        scratch_shapes=[
            pltpu.VMEM((COLS, lanes), jnp.float32),
            pltpu.VMEM((COLS, 128), jnp.float32),
            pltpu.VMEM((COLS, COLS), jnp.float32),
            pltpu.VMEM((COLS, lanes), jnp.float32),
        ],
        compiler_params=pltpu.CompilerParams(vmem_limit_bytes=16 * 2**20),
        cost_estimate=pl.CostEstimate(flops=10**7, bytes_accessed=10**6, transcendentals=0),
        name="errors",
    )(weight, codes, zeros, first_panel)


RING = (0, 1, -1, 2)
FIRST_PART = 128


def gram_kernel(total, table, a_ref, d_ref, own_ref, inv_ref, gain_rows_ref, gain_own_ref, out_ref, own):
    groups, toks = own_ref.shape[:2]

    @pl.when(pl.program_id(0) == 0)
    def _():
        for g in range(groups):
            v = own_ref[table[g]].astype(jnp.float32) * inv_ref[g] * gain_own_ref[...]
            own[g * toks : (g + 1) * toks] = v.astype(jnp.bfloat16)

    parts = []
    for g in range(groups):
        v = jnp.concatenate([a_ref[g, 0, 0], d_ref[0, g, 0]], axis=0).astype(jnp.float32)
        parts.append((v * inv_ref[g] * gain_rows_ref[0]).astype(jnp.bfloat16))
    out_ref[...] = contract_rows(jnp.concatenate(parts, axis=0), own[...]) * (1.0 / total)


def mean_outer(part_a, part_d, own, inv_norm, gain_rows, gain_own, table):
    groups, toks, feats = own.shape
    pieces = 2 * groups
    spec = pltpu.PrefetchScalarGridSpec(
        num_scalar_prefetch=1,
        grid=(pieces,),
        in_specs=[
            pl.BlockSpec((groups, 1, 1) + part_a.shape[3:], lambda i, s: (0, i // 2, i % 2, 0, 0)),
            pl.BlockSpec((1, groups, 1) + part_d.shape[3:], lambda i, s: (i // 2, 0, i % 2, 0, 0)),
            pl.BlockSpec((groups, toks, feats), lambda i, s: (0, 0, 0)),
            pl.BlockSpec((groups, toks, 1), lambda i, s: (0, 0, 0)),
            pl.BlockSpec((1, 1, feats), lambda i, s: (s[groups + i], 0, 0)),
            pl.BlockSpec((1, feats), lambda i, s: (0, 0)),
        ],
        out_specs=pl.BlockSpec((feats, feats), lambda i, s: (s[groups + i], 0)),
        scratch_shapes=[pltpu.VMEM((groups * toks, feats), jnp.bfloat16)],
    )
    return pl.pallas_call(
        functools.partial(gram_kernel, groups * toks),
        grid_spec=spec,
        out_shape=jax.ShapeDtypeStruct((pieces * feats, feats), jnp.float32),
        compiler_params=pltpu.CompilerParams(vmem_limit_bytes=32 * 2**20),
        cost_estimate=pl.CostEstimate(
            flops=2 * groups * toks * pieces * feats * feats,
            bytes_accessed=20 * 2**20,
            transcendentals=0,
        ),
        name="mean_outer",
    )(table, part_a, part_d, own, inv_norm, gain_rows.reshape(pieces, 1, feats), gain_own.reshape(1, feats))


def corrected_kernel(w_ref, e_ref, p_ref, out_ref):
    rows, feats = out_ref.shape
    correction = jnp.dot(e_ref[...].reshape(rows, COLS), p_ref[...], preferred_element_type=jnp.float32)
    value = w_ref[...].reshape(rows, feats).astype(jnp.float32) - correction
    out_ref[...] = value.astype(jnp.bfloat16)


def corrected(moved, errors, panel):
    shards, rows, feats = moved.shape
    step = 4
    return pl.pallas_call(
        corrected_kernel,
        grid=(shards // step,),
        out_shape=jax.ShapeDtypeStruct((shards * rows, feats), jnp.bfloat16),
        in_specs=[
            pl.BlockSpec((step, rows, feats), lambda i: (i, 0, 0)),
            pl.BlockSpec((step, rows, COLS), lambda i: (i, 0, 0)),
            pl.BlockSpec((COLS, feats), lambda i: (0, 0)),
        ],
        out_specs=pl.BlockSpec((step * rows, feats), lambda i: (i, 0)),
        compiler_params=pltpu.CompilerParams(vmem_limit_bytes=32 * 2**20),
        cost_estimate=pl.CostEstimate(
            flops=2 * shards * rows * feats * COLS, bytes_accessed=20 * 2**20, transcendentals=0
        ),
        name="corrected",
    )(moved, errors, panel)


def pack_kernel(w_ref, out_ref):
    feats = out_ref.shape[2]
    for i in range(out_ref.shape[0]):
        out_ref[i] = w_ref[:, i * feats : (i + 1) * feats]


def pack(weight, feats):
    rows, total = weight.shape
    shards = total // feats
    return pl.pallas_call(
        pack_kernel,
        grid=(shards // 2,),
        out_shape=jax.ShapeDtypeStruct((shards, rows, feats), weight.dtype),
        in_specs=[pl.BlockSpec((rows, 2 * feats), lambda i: (0, i))],
        out_specs=pl.BlockSpec((2, rows, feats), lambda i: (i, 0, 0)),
        cost_estimate=pl.CostEstimate(flops=0, bytes_accessed=4 * rows * total, transcendentals=0),
        name="pack",
    )(weight)


def shift(d, along_x):
    if along_x:
        return moves(lambda t, x, z, h: (t, (x + d) % 4, z, h))
    return moves(lambda t, x, z, h: (t, x, (z + d) % 4, h))


def ring(block, along_x):
    others = [lax.ppermute(block, ALL, shift(-d, along_x)) for d in RING[1:]]
    return [block] + others


def exchange(block):
    others = [lax.ppermute(block, ALL, moves(lambda t, x, z, h, k=k: (t ^ k, x, z, h))) for k in (1, 2, 3)]
    return jnp.stack([block] + others)


def later(value, *others):
    return lax.optimization_barrier((value,) + others)[0]


def first_columns(panels, t, p):
    nothing = jnp.zeros_like(panels)
    held = jnp.concatenate(
        [
            jnp.where((t == 0) & (p == 0), panels, nothing),
            jnp.where((t == 0) & (p == 1), panels, nothing),
        ],
        axis=1,
    )
    four, two = range(4), range(2)
    steps = [
        [[(index(0, 0, 0, h), index(0, 0, 0, 1 - h)) for h in two]],
        [[(index(0, 0, 0, h), index(0, x, 0, h)) for h in two] for x in (1, 2, 3)],
        [[(index(0, x, 0, h), index(0, x, z, h)) for x in four for h in two] for z in (1, 2, 3)],
        [
            [(index(0, x, z, h), index(t, x, z, h)) for x in four for z in four for h in two]
            for t in (1, 2, 3)
        ],
    ]
    return held, steps


def spread(held, perms):
    for got in [lax.ppermute(held, ALL, perm) for perm in perms]:
        held = held + got
    return held


def own_columns(panels, t):
    def target(k):
        def to(tt, x, z, h):
            i = (z % 2) * 2 + h
            return (i ^ k, tt, x, z // 2)

        return to

    got = jnp.stack([lax.ppermute(panels, ALL, moves(target(k))) for k in range(4)])
    order = [lax.dynamic_index_in_dim(got, t ^ i, 0, keepdims=False) for i in range(4)]
    return jnp.concatenate(order, axis=1)


def on_device(residual, norm_gain, weight, scale_codes, zero_points, panels):
    toks, feats = residual.shape
    rows, feat_total = weight.shape
    t = lax.axis_index("tok")
    p = lax.axis_index("tp")
    x, z, h = p // 8, p // 2 % 4, p % 2
    shards = lax.axis_size("tp")
    groups = lax.axis_size("tok")

    held, steps = first_columns(panels, t, p)
    held = spread(held, steps[0])
    both = jnp.stack(
        [
            lax.ppermute(residual, ALL, moves(lambda tt, x, z, h: (x, tt, z, h))),
            lax.ppermute(residual, ALL, moves(lambda tt, x, z, h: (x, tt, z, 1 - h))),
        ]
    )
    both, held = lax.optimization_barrier((both, held))
    held = spread(held, steps[1])
    left = toks - FIRST_PART
    part_a = jnp.concatenate(ring(both[:, :FIRST_PART], False))
    part_d = jnp.concatenate(ring(both[:, FIRST_PART:], True))
    held = spread(spread(held, steps[2]), steps[3])
    part_a, part_d, first_panel, panels, residual, weight = lax.optimization_barrier(
        (part_a, part_d, held, panels, residual, weight)
    )
    part_a = ring(part_a, True)
    part_d = ring(part_d, False)

    pad = -(-rows // 128) * 128 - rows
    codes = jnp.pad(scale_codes.astype(jnp.float32).T, ((0, 0), (0, pad)))
    zeros = jnp.pad(zero_points.astype(jnp.float32).T, ((0, 0), (0, pad)))
    errors = block_errors(weight[:, :COLS], codes, zeros, first_panel)
    packed = pack(weight, feats)
    part_a, part_d, errors, packed, panels, residual = lax.optimization_barrier(
        (part_a, part_d, errors, packed, panels, residual)
    )

    moved = lax.all_to_all(packed, "tp", split_axis=0, concat_axis=0)

    own = exchange(residual)
    own_panel = own_columns(panels, t)
    part_a = jnp.stack(part_a).reshape(4, 4, 2, FIRST_PART, feats)
    part_d = jnp.stack(part_d).reshape(4, 4, 2, left, feats)

    sums = jnp.concatenate(
        [
            jnp.sum(jnp.square(part_a.astype(jnp.float32)), axis=(1, 2, 4)),
            jnp.sum(jnp.square(part_d.astype(jnp.float32)), axis=(0, 2, 4)),
        ],
        axis=1,
    )
    sums = sums + lax.ppermute(sums, ALL, moves(lambda tt, x, z, h: (tt ^ 1, x, z, h)))
    sums = sums + lax.ppermute(sums, ALL, moves(lambda tt, x, z, h: (tt ^ 2, x, z, h)))
    copies = later(jnp.broadcast_to(errors[None], (shards, rows, COLS)), moved, own, own_panel, sums)
    errors_all = lax.all_to_all(copies, "tp", split_axis=0, concat_axis=0)
    inv_norm = lax.rsqrt(sums / feat_total + EPS)[:, :, None]
    quarter_feats = feat_total // groups
    gain_rows = lax.dynamic_slice_in_dim(norm_gain, t * quarter_feats, quarter_feats, 0)
    gain_own = lax.dynamic_slice_in_dim(norm_gain, p * feats, feats, 0)
    table = jnp.stack(
        [((x + d) % 4) ^ t for d in RING]
        + [((z + d) % 4) * 2 + (h ^ c) for d in RING for c in range(2)]
    ).astype(jnp.int32)
    gram = mean_outer(part_a, part_d, own, inv_norm, gain_rows, gain_own, table)

    return (gram, corrected(moved, errors_all, own_panel))


def solution(mesh):
    in_specs = (
        P("tok", "tp"),
        P(),
        P(("tok", "tp"), None),
        P(("tok", "tp"), None),
        P(("tok", "tp"), None),
        P(None, ("tok", "tp")),
    )
    out_specs = (P("tok", "tp"), P("tok", "tp"))
    return jax.shard_map(
        on_device, mesh=mesh, in_specs=in_specs, out_specs=out_specs, check_vma=False
    )
```

```python
import functools
import math

import jax
import jax.numpy as jnp
from jax import lax
from jax.experimental import pallas as pl
from jax.experimental.pallas import tpu as pltpu
from jax.sharding import PartitionSpec as P

BLOCK = 128
BLOCKS = 2
COLS = BLOCK * BLOCKS
SUB = 8

EPS = 1e-05
SOFTNESS = 0.9
ALL = ("tok", "tp")

SINE = tuple(
    c * SOFTNESS / (2.0 * math.pi)
    for c in (
        6.283182818496983,
        -41.341421393740156,
        81.59618374823393,
        -76.58009925759313,
        41.20538928368347,
        -12.271253496065944,
    )
)


def tp_index(x, z, h):
    return x * 8 + z * 2 + h


def index(t, x, z, h):
    return t * 32 + tp_index(x, z, h)


PLACES = [(t, x, z, h) for t in range(4) for x in range(4) for z in range(4) for h in range(2)]


def moves(fn):
    return [(index(*a), index(*fn(*a))) for a in PLACES]


def split3(v):
    hi = v.astype(jnp.bfloat16).astype(jnp.float32)
    rest = v - hi
    mid = rest.astype(jnp.bfloat16).astype(jnp.float32)
    return hi, mid, rest - mid


def contract_rows(a, b):
    return lax.dot_general(a, b, (((0,), (0,)), ((), ())), preferred_element_type=jnp.float32)


def errors_kernel(w_ref, codes_ref, zeros_ref, p_ref, e_ref, work, diag, panel, errs):
    rows = w_ref.shape[0]
    lanes = work.shape[1]
    w = w_ref[...].astype(jnp.float32)
    w = jnp.concatenate([w, jnp.zeros((lanes - rows, COLS), jnp.float32)], axis=0)
    work[...] = w.T
    panel[...] = p_ref[...].astype(jnp.float32)
    across = panel[...].T
    row_id = lax.broadcasted_iota(jnp.int32, (COLS, COLS), 0)
    col_id = lax.broadcasted_iota(jnp.int32, (COLS, COLS), 1)
    pivots = jnp.sum(jnp.where(row_id == col_id, across, 0.0), axis=1, keepdims=True)
    diag[:, SUB : SUB + 1] = 1.0 / pivots
    for g in range(COLS // SUB):
        diag[g * SUB : (g + 1) * SUB, :SUB] = across[g * SUB : (g + 1) * SUB, g * SUB : (g + 1) * SUB]
    sub_id = lax.broadcasted_iota(jnp.int32, (SUB, lanes), 0)
    for k in range(BLOCKS):
        first = k * BLOCK
        half = codes_ref[k : k + 1, :] * 0.5 - 3.0
        scale = jnp.broadcast_to(jnp.exp2(half), (SUB, lanes))
        inverse = jnp.broadcast_to(jnp.exp2(-half), (SUB, lanes))
        zero = jnp.broadcast_to(zeros_ref[k : k + 1, :], (SUB, lanes))

        def group(g, carry):
            base = pl.multiple_of(first + g * SUB, SUB)
            now = work[pl.ds(base, SUB), :]
            local = diag[pl.ds(base, SUB), :]
            inv_pivot = jnp.broadcast_to(local[:, SUB : SUB + 1], (SUB, lanes))
            found = jnp.zeros((SUB, lanes), jnp.float32)
            for i in range(SUB):
                u = now * inverse + zero
                r = u - jnp.round(u)
                r2 = r * r
                r4 = r2 * r2
                wave = (SINE[0] + SINE[1] * r2) + r4 * (
                    (SINE[2] + SINE[3] * r2) + r4 * (SINE[4] + SINE[5] * r2)
                )
                soft = jnp.clip(u - wave * r, 0.0, 15.0)
                error = (now - scale * (soft - zero)) * inv_pivot
                error = jnp.broadcast_to(error[i : i + 1, :], (SUB, lanes))
                now = now - jnp.broadcast_to(local[:, i : i + 1], (SUB, lanes)) * error
                found = jnp.where(sub_id == i, error, found)
            errs[pl.ds(base, SUB), :] = found
            p_rows = panel[pl.ds(base, SUB), first : first + BLOCK]
            p_rows = jnp.concatenate([p_rows] * 3, axis=0).astype(jnp.bfloat16)
            e_rows = jnp.concatenate(split3(found), axis=0).astype(jnp.bfloat16)
            work[first : first + BLOCK, :] -= contract_rows(p_rows, e_rows)
            return carry

        lax.fori_loop(0, BLOCK // SUB, group, 0)
        if k + 1 < BLOCKS:
            p_rows = panel[first : first + BLOCK, first + BLOCK :].astype(jnp.bfloat16)
            spill = 0.0
            for part in split3(errs[first : first + BLOCK, :]):
                spill = spill + contract_rows(p_rows, part.astype(jnp.bfloat16))
            work[first + BLOCK :, :] -= spill
    e_ref[...] = errs[...].T[:rows].astype(jnp.bfloat16)


def block_errors(weight, codes, zeros, first_panel):
    rows = weight.shape[0]
    lanes = -(-rows // 128) * 128
    return pl.pallas_call(
        errors_kernel,
        grid=(1,),
        out_shape=jax.ShapeDtypeStruct((rows, COLS), jnp.bfloat16),
        in_specs=[
            pl.BlockSpec((rows, COLS), lambda i: (0, 0)),
            pl.BlockSpec((BLOCKS, lanes), lambda i: (0, 0)),
            pl.BlockSpec((BLOCKS, lanes), lambda i: (0, 0)),
            pl.BlockSpec((COLS, COLS), lambda i: (0, 0)),
        ],
        out_specs=pl.BlockSpec((rows, COLS), lambda i: (0, 0)),
        scratch_shapes=[
            pltpu.VMEM((COLS, lanes), jnp.float32),
            pltpu.VMEM((COLS, 128), jnp.float32),
            pltpu.VMEM((COLS, COLS), jnp.float32),
            pltpu.VMEM((COLS, lanes), jnp.float32),
        ],
        compiler_params=pltpu.CompilerParams(vmem_limit_bytes=16 * 2**20),
        cost_estimate=pl.CostEstimate(flops=10**7, bytes_accessed=10**6, transcendentals=0),
        name="errors",
    )(weight, codes, zeros, first_panel)


RING = (0, 1, -1, 2)
FIRST_PART = 128


def gram_kernel(total, table, a_ref, d_ref, own_ref, inv_ref, gain_rows_ref, gain_own_ref, out_ref, own):
    groups, toks = own_ref.shape[:2]

    @pl.when(pl.program_id(0) == 0)
    def _():
        for g in range(groups):
            v = own_ref[table[g]].astype(jnp.float32) * inv_ref[g] * gain_own_ref[...]
            own[g * toks : (g + 1) * toks] = v.astype(jnp.bfloat16)

    parts = []
    for g in range(groups):
        v = jnp.concatenate([a_ref[g, 0, 0], d_ref[0, g, 0]], axis=0).astype(jnp.float32)
        parts.append((v * inv_ref[g] * gain_rows_ref[0]).astype(jnp.bfloat16))
    out_ref[...] = contract_rows(jnp.concatenate(parts, axis=0), own[...]) * (1.0 / total)


def mean_outer(part_a, part_d, own, inv_norm, gain_rows, gain_own, table):
    groups, toks, feats = own.shape
    pieces = 2 * groups
    spec = pltpu.PrefetchScalarGridSpec(
        num_scalar_prefetch=1,
        grid=(pieces,),
        in_specs=[
            pl.BlockSpec((groups, 1, 1) + part_a.shape[3:], lambda i, s: (0, i // 2, i % 2, 0, 0)),
            pl.BlockSpec((1, groups, 1) + part_d.shape[3:], lambda i, s: (i // 2, 0, i % 2, 0, 0)),
            pl.BlockSpec((groups, toks, feats), lambda i, s: (0, 0, 0)),
            pl.BlockSpec((groups, toks, 1), lambda i, s: (0, 0, 0)),
            pl.BlockSpec((1, 1, feats), lambda i, s: (s[groups + i], 0, 0)),
            pl.BlockSpec((1, feats), lambda i, s: (0, 0)),
        ],
        out_specs=pl.BlockSpec((feats, feats), lambda i, s: (s[groups + i], 0)),
        scratch_shapes=[pltpu.VMEM((groups * toks, feats), jnp.bfloat16)],
    )
    return pl.pallas_call(
        functools.partial(gram_kernel, groups * toks),
        grid_spec=spec,
        out_shape=jax.ShapeDtypeStruct((pieces * feats, feats), jnp.float32),
        compiler_params=pltpu.CompilerParams(vmem_limit_bytes=32 * 2**20),
        cost_estimate=pl.CostEstimate(
            flops=2 * groups * toks * pieces * feats * feats,
            bytes_accessed=20 * 2**20,
            transcendentals=0,
        ),
        name="mean_outer",
    )(table, part_a, part_d, own, inv_norm, gain_rows.reshape(pieces, 1, feats), gain_own.reshape(1, feats))


def corrected_kernel(w_ref, e_ref, p_ref, out_ref):
    rows, feats = out_ref.shape
    correction = jnp.dot(e_ref[...].reshape(rows, COLS), p_ref[...], preferred_element_type=jnp.float32)
    value = w_ref[...].reshape(rows, feats).astype(jnp.float32) - correction
    out_ref[...] = value.astype(jnp.bfloat16)


def corrected(moved, errors, panel):
    shards, rows, feats = moved.shape
    step = 4
    return pl.pallas_call(
        corrected_kernel,
        grid=(shards // step,),
        out_shape=jax.ShapeDtypeStruct((shards * rows, feats), jnp.bfloat16),
        in_specs=[
            pl.BlockSpec((step, rows, feats), lambda i: (i, 0, 0)),
            pl.BlockSpec((step, rows, COLS), lambda i: (i, 0, 0)),
            pl.BlockSpec((COLS, feats), lambda i: (0, 0)),
        ],
        out_specs=pl.BlockSpec((step * rows, feats), lambda i: (i, 0)),
        compiler_params=pltpu.CompilerParams(vmem_limit_bytes=32 * 2**20),
        cost_estimate=pl.CostEstimate(
            flops=2 * shards * rows * feats * COLS, bytes_accessed=20 * 2**20, transcendentals=0
        ),
        name="corrected",
    )(moved, errors, panel)


def pack_kernel(w_ref, out_ref):
    feats = out_ref.shape[2]
    for i in range(out_ref.shape[0]):
        out_ref[i] = w_ref[:, i * feats : (i + 1) * feats]


def pack(weight, feats):
    rows, total = weight.shape
    shards = total // feats
    return pl.pallas_call(
        pack_kernel,
        grid=(shards // 2,),
        out_shape=jax.ShapeDtypeStruct((shards, rows, feats), weight.dtype),
        in_specs=[pl.BlockSpec((rows, 2 * feats), lambda i: (0, i))],
        out_specs=pl.BlockSpec((2, rows, feats), lambda i: (i, 0, 0)),
        cost_estimate=pl.CostEstimate(flops=0, bytes_accessed=4 * rows * total, transcendentals=0),
        name="pack",
    )(weight)


def shift(d, along_x):
    if along_x:
        return moves(lambda t, x, z, h: (t, (x + d) % 4, z, h))
    return moves(lambda t, x, z, h: (t, x, (z + d) % 4, h))


def ring(block, along_x):
    others = [lax.ppermute(block, ALL, shift(-d, along_x)) for d in RING[1:]]
    return [block] + others


def beside(block):
    return jnp.stack([block, lax.ppermute(block, ALL, moves(lambda t, x, z, h: (t ^ 1, x, z, h)))])


def beyond(pair):
    return jnp.concatenate([pair, lax.ppermute(pair, ALL, moves(lambda t, x, z, h: (t ^ 2, x, z, h)))])


def later(value, *others):
    return lax.optimization_barrier((value,) + others)[0]


def first_columns(panels, t, p):
    nothing = jnp.zeros_like(panels)
    held = jnp.concatenate(
        [
            jnp.where((t == 0) & (p == 0), panels, nothing),
            jnp.where((t == 0) & (p == 1), panels, nothing),
        ],
        axis=1,
    )
    four, two = range(4), range(2)
    steps = [
        [[(index(0, 0, 0, h), index(0, 0, 0, 1 - h)) for h in two]],
        [[(index(0, 0, 0, h), index(0, x, 0, h)) for h in two] for x in (1, 2, 3)],
        [[(index(0, x, 0, h), index(0, x, z, h)) for x in four for h in two] for z in (1, 2, 3)],
        [
            [(index(0, x, z, h), index(t, x, z, h)) for x in four for z in four for h in two]
            for t in (1, 2, 3)
        ],
    ]
    return held, steps


def spread(held, perms):
    for got in [lax.ppermute(held, ALL, perm) for perm in perms]:
        held = held + got
    return held


def on_device(residual, norm_gain, weight, scale_codes, zero_points, panels):
    toks, feats = residual.shape
    rows, feat_total = weight.shape
    t = lax.axis_index("tok")
    p = lax.axis_index("tp")
    x, z, h = p // 8, p // 2 % 4, p % 2
    shards = lax.axis_size("tp")
    groups = lax.axis_size("tok")

    held, steps = first_columns(panels, t, p)
    held = spread(held, steps[0])
    both = jnp.stack(
        [
            lax.ppermute(residual, ALL, moves(lambda tt, x, z, h: (x, tt, z, h))),
            lax.ppermute(residual, ALL, moves(lambda tt, x, z, h: (x, tt, z, 1 - h))),
        ]
    )
    shard = lax.ppermute(panels, ALL, moves(lambda tt, x, z, h: (z % 2 * 2 + h, tt, x, z // 2)))
    both, held, shard = lax.optimization_barrier((both, held, shard))
    held = spread(held, steps[1])
    left = toks - FIRST_PART
    part_a = jnp.concatenate(ring(both[:, :FIRST_PART], False))
    part_d = jnp.concatenate(ring(both[:, FIRST_PART:], True))
    held = spread(spread(held, steps[2]), steps[3])
    part_a, part_d, first_panel, shard, residual, weight = lax.optimization_barrier(
        (part_a, part_d, held, shard, residual, weight)
    )
    part_a = ring(part_a, True)
    part_d = ring(part_d, False)

    pad = -(-rows // 128) * 128 - rows
    codes = jnp.pad(scale_codes.astype(jnp.float32).T, ((0, 0), (0, pad)))
    zeros = jnp.pad(zero_points.astype(jnp.float32).T, ((0, 0), (0, pad)))
    errors = block_errors(weight[:, :COLS], codes, zeros, first_panel)
    packed = pack(weight, feats)
    part_a, part_d, errors, packed, shard, residual = lax.optimization_barrier(
        (part_a, part_d, errors, packed, shard, residual)
    )

    moved = lax.all_to_all(packed, "tp", split_axis=0, concat_axis=0)

    pair = beside(jnp.concatenate([residual, shard], axis=1))
    met = beyond(pair)
    own = met[:, :, :feats]
    own_panel = jnp.concatenate(
        [lax.dynamic_index_in_dim(met, t ^ i, 0, keepdims=False)[:, feats:] for i in range(groups)], axis=1
    )
    part_a = jnp.stack(part_a).reshape(4, 4, 2, FIRST_PART, feats)
    part_d = jnp.stack(part_d).reshape(4, 4, 2, left, feats)

    sums = jnp.concatenate(
        [
            jnp.sum(jnp.square(part_a.astype(jnp.float32)), axis=(1, 2, 4)),
            jnp.sum(jnp.square(part_d.astype(jnp.float32)), axis=(0, 2, 4)),
        ],
        axis=1,
    )
    sums = sums + lax.ppermute(sums, ALL, moves(lambda tt, x, z, h: (tt ^ 1, x, z, h)))
    sums = sums + lax.ppermute(sums, ALL, moves(lambda tt, x, z, h: (tt ^ 2, x, z, h)))
    copies = later(jnp.broadcast_to(errors[None], (shards, rows, COLS)), moved, met, sums)
    errors_all = lax.all_to_all(copies, "tp", split_axis=0, concat_axis=0)
    inv_norm = lax.rsqrt(sums / feat_total + EPS)[:, :, None]
    quarter_feats = feat_total // groups
    gain_rows = lax.dynamic_slice_in_dim(norm_gain, t * quarter_feats, quarter_feats, 0)
    gain_own = lax.dynamic_slice_in_dim(norm_gain, p * feats, feats, 0)
    table = jnp.stack(
        [((x + d) % 4) ^ t for d in RING]
        + [((z + d) % 4) * 2 + (h ^ c) for d in RING for c in range(2)]
    ).astype(jnp.int32)
    gram = mean_outer(part_a, part_d, own, inv_norm, gain_rows, gain_own, table)

    return (gram, corrected(moved, errors_all, own_panel))


def solution(mesh):
    in_specs = (
        P("tok", "tp"),
        P(),
        P(("tok", "tp"), None),
        P(("tok", "tp"), None),
        P(("tok", "tp"), None),
        P(None, ("tok", "tp")),
    )
    out_specs = (P("tok", "tp"), P("tok", "tp"))
    return jax.shard_map(
        on_device, mesh=mesh, in_specs=in_specs, out_specs=out_specs, check_vma=False
    )
```

```python
import functools
import math

import jax
import jax.numpy as jnp
from jax import lax
from jax.experimental import pallas as pl
from jax.experimental.pallas import tpu as pltpu
from jax.sharding import PartitionSpec as P

BLOCK = 128
BLOCKS = 2
COLS = BLOCK * BLOCKS
SUB = 8

EPS = 1e-05
SOFTNESS = 0.9
ALL = ("tok", "tp")

SINE = tuple(
    c * SOFTNESS / (2.0 * math.pi)
    for c in (
        6.283182818496983,
        -41.341421393740156,
        81.59618374823393,
        -76.58009925759313,
        41.20538928368347,
        -12.271253496065944,
    )
)


def tp_index(x, z, h):
    return x * 8 + z * 2 + h


def index(t, x, z, h):
    return t * 32 + tp_index(x, z, h)


PLACES = [(t, x, z, h) for t in range(4) for x in range(4) for z in range(4) for h in range(2)]


def moves(fn):
    return [(index(*a), index(*fn(*a))) for a in PLACES]


def split3(v):
    hi = v.astype(jnp.bfloat16).astype(jnp.float32)
    rest = v - hi
    mid = rest.astype(jnp.bfloat16).astype(jnp.float32)
    return hi, mid, rest - mid


def contract_rows(a, b):
    return lax.dot_general(a, b, (((0,), (0,)), ((), ())), preferred_element_type=jnp.float32)


def errors_kernel(w_ref, codes_ref, zeros_ref, p_ref, e_ref, work, diag, panel, errs):
    rows = w_ref.shape[0]
    lanes = work.shape[1]
    w = w_ref[...].astype(jnp.float32)
    w = jnp.concatenate([w, jnp.zeros((lanes - rows, COLS), jnp.float32)], axis=0)
    work[...] = w.T
    panel[...] = p_ref[...].astype(jnp.float32)
    across = panel[...].T
    row_id = lax.broadcasted_iota(jnp.int32, (COLS, COLS), 0)
    col_id = lax.broadcasted_iota(jnp.int32, (COLS, COLS), 1)
    pivots = jnp.sum(jnp.where(row_id == col_id, across, 0.0), axis=1, keepdims=True)
    diag[:, SUB : SUB + 1] = 1.0 / pivots
    for g in range(COLS // SUB):
        diag[g * SUB : (g + 1) * SUB, :SUB] = across[g * SUB : (g + 1) * SUB, g * SUB : (g + 1) * SUB]
    sub_id = lax.broadcasted_iota(jnp.int32, (SUB, lanes), 0)
    for k in range(BLOCKS):
        first = k * BLOCK
        half = codes_ref[k : k + 1, :] * 0.5 - 3.0
        scale = jnp.broadcast_to(jnp.exp2(half), (SUB, lanes))
        inverse = jnp.broadcast_to(jnp.exp2(-half), (SUB, lanes))
        zero = jnp.broadcast_to(zeros_ref[k : k + 1, :], (SUB, lanes))

        def group(g, carry):
            base = pl.multiple_of(first + g * SUB, SUB)
            now = work[pl.ds(base, SUB), :]
            local = diag[pl.ds(base, SUB), :]
            inv_pivot = jnp.broadcast_to(local[:, SUB : SUB + 1], (SUB, lanes))
            found = jnp.zeros((SUB, lanes), jnp.float32)
            for i in range(SUB):
                u = now * inverse + zero
                r = u - jnp.round(u)
                r2 = r * r
                r4 = r2 * r2
                wave = (SINE[0] + SINE[1] * r2) + r4 * (
                    (SINE[2] + SINE[3] * r2) + r4 * (SINE[4] + SINE[5] * r2)
                )
                soft = jnp.clip(u - wave * r, 0.0, 15.0)
                error = (now - scale * (soft - zero)) * inv_pivot
                error = jnp.broadcast_to(error[i : i + 1, :], (SUB, lanes))
                now = now - jnp.broadcast_to(local[:, i : i + 1], (SUB, lanes)) * error
                found = jnp.where(sub_id == i, error, found)
            errs[pl.ds(base, SUB), :] = found
            p_rows = panel[pl.ds(base, SUB), first : first + BLOCK]
            p_rows = jnp.concatenate([p_rows] * 3, axis=0).astype(jnp.bfloat16)
            e_rows = jnp.concatenate(split3(found), axis=0).astype(jnp.bfloat16)
            work[first : first + BLOCK, :] -= contract_rows(p_rows, e_rows)
            return carry

        lax.fori_loop(0, BLOCK // SUB, group, 0)
        if k + 1 < BLOCKS:
            p_rows = panel[first : first + BLOCK, first + BLOCK :].astype(jnp.bfloat16)
            spill = 0.0
            for part in split3(errs[first : first + BLOCK, :]):
                spill = spill + contract_rows(p_rows, part.astype(jnp.bfloat16))
            work[first + BLOCK :, :] -= spill
    e_ref[...] = errs[...].T[:rows].astype(jnp.bfloat16)


def block_errors(weight, codes, zeros, first_panel):
    rows = weight.shape[0]
    lanes = -(-rows // 128) * 128
    return pl.pallas_call(
        errors_kernel,
        grid=(1,),
        out_shape=jax.ShapeDtypeStruct((rows, COLS), jnp.bfloat16),
        in_specs=[
            pl.BlockSpec((rows, COLS), lambda i: (0, 0)),
            pl.BlockSpec((BLOCKS, lanes), lambda i: (0, 0)),
            pl.BlockSpec((BLOCKS, lanes), lambda i: (0, 0)),
            pl.BlockSpec((COLS, COLS), lambda i: (0, 0)),
        ],
        out_specs=pl.BlockSpec((rows, COLS), lambda i: (0, 0)),
        scratch_shapes=[
            pltpu.VMEM((COLS, lanes), jnp.float32),
            pltpu.VMEM((COLS, 128), jnp.float32),
            pltpu.VMEM((COLS, COLS), jnp.float32),
            pltpu.VMEM((COLS, lanes), jnp.float32),
        ],
        compiler_params=pltpu.CompilerParams(vmem_limit_bytes=16 * 2**20),
        cost_estimate=pl.CostEstimate(flops=10**7, bytes_accessed=10**6, transcendentals=0),
        name="errors",
    )(weight, codes, zeros, first_panel)


RING = (0, 1, -1, 2)
FIRST_PART = 128


def gram_kernel(total, table, a_ref, d_ref, own_ref, inv_ref, gain_rows_ref, gain_own_ref, out_ref, own):
    groups, toks = own_ref.shape[:2]

    @pl.when(pl.program_id(0) == 0)
    def _():
        for g in range(groups):
            v = own_ref[table[g]].astype(jnp.float32) * inv_ref[g] * gain_own_ref[...]
            own[g * toks : (g + 1) * toks] = v.astype(jnp.bfloat16)

    parts = []
    for g in range(groups):
        v = jnp.concatenate([a_ref[g, 0, 0], d_ref[0, g, 0]], axis=0).astype(jnp.float32)
        parts.append((v * inv_ref[g] * gain_rows_ref[0]).astype(jnp.bfloat16))
    out_ref[...] = contract_rows(jnp.concatenate(parts, axis=0), own[...]) * (1.0 / total)


def mean_outer(part_a, part_d, own, inv_norm, gain_rows, gain_own, table):
    groups, toks, feats = own.shape
    pieces = 2 * groups
    spec = pltpu.PrefetchScalarGridSpec(
        num_scalar_prefetch=1,
        grid=(pieces,),
        in_specs=[
            pl.BlockSpec((groups, 1, 1) + part_a.shape[3:], lambda i, s: (0, i // 2, i % 2, 0, 0)),
            pl.BlockSpec((1, groups, 1) + part_d.shape[3:], lambda i, s: (i // 2, 0, i % 2, 0, 0)),
            pl.BlockSpec((groups, toks, feats), lambda i, s: (0, 0, 0)),
            pl.BlockSpec((groups, toks, 1), lambda i, s: (0, 0, 0)),
            pl.BlockSpec((1, 1, feats), lambda i, s: (s[groups + i], 0, 0)),
            pl.BlockSpec((1, feats), lambda i, s: (0, 0)),
        ],
        out_specs=pl.BlockSpec((feats, feats), lambda i, s: (s[groups + i], 0)),
        scratch_shapes=[pltpu.VMEM((groups * toks, feats), jnp.bfloat16)],
    )
    return pl.pallas_call(
        functools.partial(gram_kernel, groups * toks),
        grid_spec=spec,
        out_shape=jax.ShapeDtypeStruct((pieces * feats, feats), jnp.float32),
        compiler_params=pltpu.CompilerParams(vmem_limit_bytes=32 * 2**20),
        cost_estimate=pl.CostEstimate(
            flops=2 * groups * toks * pieces * feats * feats,
            bytes_accessed=20 * 2**20,
            transcendentals=0,
        ),
        name="mean_outer",
    )(table, part_a, part_d, own, inv_norm, gain_rows.reshape(pieces, 1, feats), gain_own.reshape(1, feats))


def corrected_kernel(feats, both_ref, p_ref, out_ref):
    rows = out_ref.shape[0]
    errors = both_ref[:, :, feats:].reshape(rows, COLS)
    correction = jnp.dot(errors, p_ref[...], preferred_element_type=jnp.float32)
    value = both_ref[:, :, :feats].reshape(rows, feats).astype(jnp.float32) - correction
    out_ref[...] = value.astype(jnp.bfloat16)


def corrected(arrived, panel):
    shards, rows, width = arrived.shape
    feats = width - COLS
    step = 4
    return pl.pallas_call(
        functools.partial(corrected_kernel, feats),
        grid=(shards // step,),
        out_shape=jax.ShapeDtypeStruct((shards * rows, feats), jnp.bfloat16),
        in_specs=[
            pl.BlockSpec((step, rows, width), lambda i: (i, 0, 0)),
            pl.BlockSpec((COLS, feats), lambda i: (0, 0)),
        ],
        out_specs=pl.BlockSpec((step * rows, feats), lambda i: (i, 0)),
        compiler_params=pltpu.CompilerParams(vmem_limit_bytes=32 * 2**20),
        cost_estimate=pl.CostEstimate(
            flops=2 * shards * rows * feats * COLS, bytes_accessed=20 * 2**20, transcendentals=0
        ),
        name="corrected",
    )(arrived, panel)


def pack_kernel(feats, w_ref, e_ref, out_ref):
    for i in range(out_ref.shape[0]):
        out_ref[i, :, :feats] = w_ref[:, i * feats : (i + 1) * feats]
        out_ref[i, :, feats:] = e_ref[...]


def pack(weight, errors, feats):
    rows, total = weight.shape
    shards = total // feats
    step = 2
    return pl.pallas_call(
        functools.partial(pack_kernel, feats),
        grid=(shards // step,),
        out_shape=jax.ShapeDtypeStruct((shards, rows, feats + COLS), weight.dtype),
        in_specs=[
            pl.BlockSpec((rows, step * feats), lambda i: (0, i)),
            pl.BlockSpec((rows, COLS), lambda i: (0, 0)),
        ],
        out_specs=pl.BlockSpec((step, rows, feats + COLS), lambda i: (i, 0, 0)),
        compiler_params=pltpu.CompilerParams(vmem_limit_bytes=16 * 2**20),
        cost_estimate=pl.CostEstimate(flops=0, bytes_accessed=5 * rows * total, transcendentals=0),
        name="pack",
    )(weight, errors)


def shift(d, along_x):
    if along_x:
        return moves(lambda t, x, z, h: (t, (x + d) % 4, z, h))
    return moves(lambda t, x, z, h: (t, x, (z + d) % 4, h))


def ring(block, along_x):
    others = [lax.ppermute(block, ALL, shift(-d, along_x)) for d in RING[1:]]
    return [block] + others


def beside(block):
    return jnp.stack([block, lax.ppermute(block, ALL, moves(lambda t, x, z, h: (t ^ 1, x, z, h)))])


def beyond(pair):
    return jnp.concatenate([pair, lax.ppermute(pair, ALL, moves(lambda t, x, z, h: (t ^ 2, x, z, h)))])


def later(value, *others):
    return lax.optimization_barrier((value,) + others)[0]


def first_columns(panels, t, p):
    nothing = jnp.zeros_like(panels)
    held = jnp.concatenate(
        [
            jnp.where((t == 0) & (p == 0), panels, nothing),
            jnp.where((t == 0) & (p == 1), panels, nothing),
        ],
        axis=1,
    )
    four, two = range(4), range(2)
    steps = [
        [[(index(0, 0, 0, h), index(0, 0, 0, 1 - h)) for h in two]],
        [[(index(0, 0, 0, h), index(0, x, 0, h)) for h in two] for x in (1, 2, 3)],
        [[(index(0, x, 0, h), index(0, x, z, h)) for x in four for h in two] for z in (1, 2, 3)],
        [
            [(index(0, x, z, h), index(t, x, z, h)) for x in four for z in four for h in two]
            for t in (1, 2, 3)
        ],
    ]
    return held, steps


def spread(held, perms):
    for got in [lax.ppermute(held, ALL, perm) for perm in perms]:
        held = held + got
    return held


def on_device(residual, norm_gain, weight, scale_codes, zero_points, panels):
    toks, feats = residual.shape
    rows, feat_total = weight.shape
    t = lax.axis_index("tok")
    p = lax.axis_index("tp")
    x, z, h = p // 8, p // 2 % 4, p % 2
    shards = lax.axis_size("tp")
    groups = lax.axis_size("tok")

    held, steps = first_columns(panels, t, p)
    held = spread(held, steps[0])
    both = jnp.stack(
        [
            lax.ppermute(residual, ALL, moves(lambda tt, x, z, h: (x, tt, z, h))),
            lax.ppermute(residual, ALL, moves(lambda tt, x, z, h: (x, tt, z, 1 - h))),
        ]
    )
    shard = lax.ppermute(panels, ALL, moves(lambda tt, x, z, h: (z % 2 * 2 + h, tt, x, z // 2)))
    both, held, shard = lax.optimization_barrier((both, held, shard))
    held = spread(held, steps[1])
    left = toks - FIRST_PART
    part_a = jnp.concatenate(ring(both[:, :FIRST_PART], False))
    part_d = jnp.concatenate(ring(both[:, FIRST_PART:], True))
    held = spread(spread(held, steps[2]), steps[3])
    part_a, part_d, first_panel, shard, residual, weight = lax.optimization_barrier(
        (part_a, part_d, held, shard, residual, weight)
    )
    part_a = ring(part_a, True)
    part_d = ring(part_d, False)

    pad = -(-rows // 128) * 128 - rows
    codes = jnp.pad(scale_codes.astype(jnp.float32).T, ((0, 0), (0, pad)))
    zeros = jnp.pad(zero_points.astype(jnp.float32).T, ((0, 0), (0, pad)))
    errors = block_errors(weight[:, :COLS], codes, zeros, first_panel)
    packed = pack(weight, errors, feats)
    part_a, part_d, packed, shard, residual = lax.optimization_barrier(
        (part_a, part_d, packed, shard, residual)
    )

    arrived = lax.all_to_all(packed, "tp", split_axis=0, concat_axis=0)

    pair = beside(jnp.concatenate([residual, shard], axis=1))
    met = beyond(pair)
    own = met[:, :, :feats]
    own_panel = jnp.concatenate(
        [lax.dynamic_index_in_dim(met, t ^ i, 0, keepdims=False)[:, feats:] for i in range(groups)], axis=1
    )
    part_a = jnp.stack(part_a).reshape(4, 4, 2, FIRST_PART, feats)
    part_d = jnp.stack(part_d).reshape(4, 4, 2, left, feats)

    sums = jnp.concatenate(
        [
            jnp.sum(jnp.square(part_a.astype(jnp.float32)), axis=(1, 2, 4)),
            jnp.sum(jnp.square(part_d.astype(jnp.float32)), axis=(0, 2, 4)),
        ],
        axis=1,
    )
    sums = sums + lax.ppermute(sums, ALL, moves(lambda tt, x, z, h: (tt ^ 1, x, z, h)))
    sums = sums + lax.ppermute(sums, ALL, moves(lambda tt, x, z, h: (tt ^ 2, x, z, h)))
    inv_norm = lax.rsqrt(sums / feat_total + EPS)[:, :, None]
    quarter_feats = feat_total // groups
    gain_rows = lax.dynamic_slice_in_dim(norm_gain, t * quarter_feats, quarter_feats, 0)
    gain_own = lax.dynamic_slice_in_dim(norm_gain, p * feats, feats, 0)
    table = jnp.stack(
        [((x + d) % 4) ^ t for d in RING]
        + [((z + d) % 4) * 2 + (h ^ c) for d in RING for c in range(2)]
    ).astype(jnp.int32)
    gram = mean_outer(part_a, part_d, own, inv_norm, gain_rows, gain_own, table)

    return (gram, corrected(arrived, own_panel))


def solution(mesh):
    in_specs = (
        P("tok", "tp"),
        P(),
        P(("tok", "tp"), None),
        P(("tok", "tp"), None),
        P(("tok", "tp"), None),
        P(None, ("tok", "tp")),
    )
    out_specs = (P("tok", "tp"), P("tok", "tp"))
    return jax.shard_map(
        on_device, mesh=mesh, in_specs=in_specs, out_specs=out_specs, check_vma=False
    )
```

```python
import functools
import math

import jax
import jax.numpy as jnp
from jax import lax
from jax.experimental import pallas as pl
from jax.experimental.pallas import tpu as pltpu
from jax.sharding import PartitionSpec as P

BLOCK = 128
BLOCKS = 2
COLS = BLOCK * BLOCKS
SUB = 8

EPS = 1e-05
SOFTNESS = 0.9
ALL = ("tok", "tp")

SINE = tuple(
    c * SOFTNESS / (2.0 * math.pi)
    for c in (
        6.283182818496983,
        -41.341421393740156,
        81.59618374823393,
        -76.58009925759313,
        41.20538928368347,
        -12.271253496065944,
    )
)


def tp_index(x, z, h):
    return x * 8 + z * 2 + h


def index(t, x, z, h):
    return t * 32 + tp_index(x, z, h)


PLACES = [(t, x, z, h) for t in range(4) for x in range(4) for z in range(4) for h in range(2)]


def moves(fn):
    return [(index(*a), index(*fn(*a))) for a in PLACES]


def split3(v):
    hi = v.astype(jnp.bfloat16).astype(jnp.float32)
    rest = v - hi
    mid = rest.astype(jnp.bfloat16).astype(jnp.float32)
    return hi, mid, rest - mid


def contract_rows(a, b):
    return lax.dot_general(a, b, (((0,), (0,)), ((), ())), preferred_element_type=jnp.float32)


def errors_kernel(w_ref, codes_ref, zeros_ref, p_ref, e_ref, work, diag, panel, errs):
    rows = w_ref.shape[0]
    lanes = work.shape[1]
    w = w_ref[...].astype(jnp.float32)
    w = jnp.concatenate([w, jnp.zeros((lanes - rows, COLS), jnp.float32)], axis=0)
    work[...] = w.T
    panel[...] = p_ref[...].astype(jnp.float32)
    across = panel[...].T
    row_id = lax.broadcasted_iota(jnp.int32, (COLS, COLS), 0)
    col_id = lax.broadcasted_iota(jnp.int32, (COLS, COLS), 1)
    pivots = jnp.sum(jnp.where(row_id == col_id, across, 0.0), axis=1, keepdims=True)
    diag[:, SUB : SUB + 1] = 1.0 / pivots
    for g in range(COLS // SUB):
        diag[g * SUB : (g + 1) * SUB, :SUB] = across[g * SUB : (g + 1) * SUB, g * SUB : (g + 1) * SUB]
    sub_id = lax.broadcasted_iota(jnp.int32, (SUB, lanes), 0)
    for k in range(BLOCKS):
        first = k * BLOCK
        half = codes_ref[k : k + 1, :] * 0.5 - 3.0
        scale = jnp.broadcast_to(jnp.exp2(half), (SUB, lanes))
        inverse = jnp.broadcast_to(jnp.exp2(-half), (SUB, lanes))
        zero = jnp.broadcast_to(zeros_ref[k : k + 1, :], (SUB, lanes))

        def group(g, carry):
            base = pl.multiple_of(first + g * SUB, SUB)
            now = work[pl.ds(base, SUB), :]
            local = diag[pl.ds(base, SUB), :]
            inv_pivot = jnp.broadcast_to(local[:, SUB : SUB + 1], (SUB, lanes))
            found = jnp.zeros((SUB, lanes), jnp.float32)
            for i in range(SUB):
                u = now * inverse + zero
                r = u - jnp.round(u)
                r2 = r * r
                r4 = r2 * r2
                wave = (SINE[0] + SINE[1] * r2) + r4 * (
                    (SINE[2] + SINE[3] * r2) + r4 * (SINE[4] + SINE[5] * r2)
                )
                soft = jnp.clip(u - wave * r, 0.0, 15.0)
                error = (now - scale * (soft - zero)) * inv_pivot
                error = jnp.broadcast_to(error[i : i + 1, :], (SUB, lanes))
                now = now - jnp.broadcast_to(local[:, i : i + 1], (SUB, lanes)) * error
                found = jnp.where(sub_id == i, error, found)
            errs[pl.ds(base, SUB), :] = found
            p_rows = panel[pl.ds(base, SUB), first : first + BLOCK]
            p_rows = jnp.concatenate([p_rows] * 3, axis=0).astype(jnp.bfloat16)
            e_rows = jnp.concatenate(split3(found), axis=0).astype(jnp.bfloat16)
            work[first : first + BLOCK, :] -= contract_rows(p_rows, e_rows)
            return carry

        lax.fori_loop(0, BLOCK // SUB, group, 0)
        if k + 1 < BLOCKS:
            p_rows = panel[first : first + BLOCK, first + BLOCK :].astype(jnp.bfloat16)
            spill = 0.0
            for part in split3(errs[first : first + BLOCK, :]):
                spill = spill + contract_rows(p_rows, part.astype(jnp.bfloat16))
            work[first + BLOCK :, :] -= spill
    e_ref[...] = errs[...].T[:rows].astype(jnp.bfloat16)


def block_errors(weight, codes, zeros, first_panel):
    rows = weight.shape[0]
    lanes = -(-rows // 128) * 128
    return pl.pallas_call(
        errors_kernel,
        grid=(1,),
        out_shape=jax.ShapeDtypeStruct((rows, COLS), jnp.bfloat16),
        in_specs=[
            pl.BlockSpec((rows, COLS), lambda i: (0, 0)),
            pl.BlockSpec((BLOCKS, lanes), lambda i: (0, 0)),
            pl.BlockSpec((BLOCKS, lanes), lambda i: (0, 0)),
            pl.BlockSpec((COLS, COLS), lambda i: (0, 0)),
        ],
        out_specs=pl.BlockSpec((rows, COLS), lambda i: (0, 0)),
        scratch_shapes=[
            pltpu.VMEM((COLS, lanes), jnp.float32),
            pltpu.VMEM((COLS, 128), jnp.float32),
            pltpu.VMEM((COLS, COLS), jnp.float32),
            pltpu.VMEM((COLS, lanes), jnp.float32),
        ],
        compiler_params=pltpu.CompilerParams(vmem_limit_bytes=16 * 2**20),
        cost_estimate=pl.CostEstimate(flops=10**7, bytes_accessed=10**6, transcendentals=0),
        name="errors",
    )(weight, codes, zeros, first_panel)


RING = (0, 1, -1, 2)
FIRST_PART = 128


def gram_kernel(total, table, a_ref, d_ref, own_ref, inv_ref, gain_rows_ref, gain_own_ref, out_ref, own):
    groups, toks = own_ref.shape[:2]

    @pl.when(pl.program_id(0) == 0)
    def _():
        for g in range(groups):
            v = own_ref[table[g]].astype(jnp.float32) * inv_ref[g] * gain_own_ref[...]
            own[g * toks : (g + 1) * toks] = v.astype(jnp.bfloat16)

    parts = []
    for g in range(groups):
        v = jnp.concatenate([a_ref[g, 0, 0], d_ref[0, g, 0]], axis=0).astype(jnp.float32)
        parts.append((v * inv_ref[g] * gain_rows_ref[0]).astype(jnp.bfloat16))
    out_ref[...] = contract_rows(jnp.concatenate(parts, axis=0), own[...]) * (1.0 / total)


def mean_outer(part_a, part_d, own, inv_norm, gain_rows, gain_own, table):
    groups, toks, feats = own.shape
    pieces = 2 * groups
    spec = pltpu.PrefetchScalarGridSpec(
        num_scalar_prefetch=1,
        grid=(pieces,),
        in_specs=[
            pl.BlockSpec((groups, 1, 1) + part_a.shape[3:], lambda i, s: (0, i // 2, i % 2, 0, 0)),
            pl.BlockSpec((1, groups, 1) + part_d.shape[3:], lambda i, s: (i // 2, 0, i % 2, 0, 0)),
            pl.BlockSpec((groups, toks, feats), lambda i, s: (0, 0, 0)),
            pl.BlockSpec((groups, toks, 1), lambda i, s: (0, 0, 0)),
            pl.BlockSpec((1, 1, feats), lambda i, s: (s[groups + i], 0, 0)),
            pl.BlockSpec((1, feats), lambda i, s: (0, 0)),
        ],
        out_specs=pl.BlockSpec((feats, feats), lambda i, s: (s[groups + i], 0)),
        scratch_shapes=[pltpu.VMEM((groups * toks, feats), jnp.bfloat16)],
    )
    return pl.pallas_call(
        functools.partial(gram_kernel, groups * toks),
        grid_spec=spec,
        out_shape=jax.ShapeDtypeStruct((pieces * feats, feats), jnp.float32),
        compiler_params=pltpu.CompilerParams(vmem_limit_bytes=32 * 2**20),
        cost_estimate=pl.CostEstimate(
            flops=2 * groups * toks * pieces * feats * feats,
            bytes_accessed=20 * 2**20,
            transcendentals=0,
        ),
        name="mean_outer",
    )(table, part_a, part_d, own, inv_norm, gain_rows.reshape(pieces, 1, feats), gain_own.reshape(1, feats))


def corrected_kernel(w_ref, e_ref, p_ref, out_ref):
    rows, feats = out_ref.shape
    correction = jnp.dot(e_ref[...].reshape(rows, COLS), p_ref[...], preferred_element_type=jnp.float32)
    value = w_ref[...].reshape(rows, feats).astype(jnp.float32) - correction
    out_ref[...] = value.astype(jnp.bfloat16)


def corrected(moved, errors, panel):
    shards, rows, feats = moved.shape
    step = 4
    return pl.pallas_call(
        corrected_kernel,
        grid=(shards // step,),
        out_shape=jax.ShapeDtypeStruct((shards * rows, feats), jnp.bfloat16),
        in_specs=[
            pl.BlockSpec((step, rows, feats), lambda i: (i, 0, 0)),
            pl.BlockSpec((step, rows, COLS), lambda i: (i, 0, 0)),
            pl.BlockSpec((COLS, feats), lambda i: (0, 0)),
        ],
        out_specs=pl.BlockSpec((step * rows, feats), lambda i: (i, 0)),
        compiler_params=pltpu.CompilerParams(vmem_limit_bytes=32 * 2**20),
        cost_estimate=pl.CostEstimate(
            flops=2 * shards * rows * feats * COLS, bytes_accessed=20 * 2**20, transcendentals=0
        ),
        name="corrected",
    )(moved, errors, panel)


def pack_kernel(w_ref, out_ref):
    feats = out_ref.shape[2]
    for i in range(out_ref.shape[0]):
        out_ref[i] = w_ref[:, i * feats : (i + 1) * feats]


def pack(weight, feats):
    rows, total = weight.shape
    shards = total // feats
    return pl.pallas_call(
        pack_kernel,
        grid=(shards // 2,),
        out_shape=jax.ShapeDtypeStruct((shards, rows, feats), weight.dtype),
        in_specs=[pl.BlockSpec((rows, 2 * feats), lambda i: (0, i))],
        out_specs=pl.BlockSpec((2, rows, feats), lambda i: (i, 0, 0)),
        cost_estimate=pl.CostEstimate(flops=0, bytes_accessed=4 * rows * total, transcendentals=0),
        name="pack",
    )(weight)


def shift(d, along_x):
    if along_x:
        return moves(lambda t, x, z, h: (t, (x + d) % 4, z, h))
    return moves(lambda t, x, z, h: (t, x, (z + d) % 4, h))


def ring(block, along_x):
    others = [lax.ppermute(block, ALL, shift(-d, along_x)) for d in RING[1:]]
    return [block] + others


def beside(block):
    return jnp.stack([block, lax.ppermute(block, ALL, moves(lambda t, x, z, h: (t ^ 1, x, z, h)))])


def beyond(pair):
    return jnp.concatenate([pair, lax.ppermute(pair, ALL, moves(lambda t, x, z, h: (t ^ 2, x, z, h)))])


def later(value, *others):
    return lax.optimization_barrier((value,) + others)[0]


def first_columns(panels, t, p):
    nothing = jnp.zeros_like(panels)
    held = jnp.concatenate(
        [
            jnp.where((t == 0) & (p == 0), panels, nothing),
            jnp.where((t == 0) & (p == 1), panels, nothing),
        ],
        axis=1,
    )
    four, two = range(4), range(2)
    steps = [
        [[(index(0, 0, 0, h), index(0, 0, 0, 1 - h)) for h in two]],
        [[(index(0, 0, 0, h), index(0, x, 0, h)) for h in two] for x in (1, 2, 3)],
        [[(index(0, x, 0, h), index(0, x, z, h)) for x in four for h in two] for z in (1, 2, 3)],
        [
            [(index(0, x, z, h), index(t, x, z, h)) for x in four for z in four for h in two]
            for t in (1, 2, 3)
        ],
    ]
    return held, steps


def spread(held, perms):
    for got in [lax.ppermute(held, ALL, perm) for perm in perms]:
        held = held + got
    return held


def on_device(residual, norm_gain, weight, scale_codes, zero_points, panels):
    toks, feats = residual.shape
    rows, feat_total = weight.shape
    t = lax.axis_index("tok")
    p = lax.axis_index("tp")
    x, z, h = p // 8, p // 2 % 4, p % 2
    shards = lax.axis_size("tp")
    groups = lax.axis_size("tok")

    held, steps = first_columns(panels, t, p)
    held = spread(held, steps[0])
    both = jnp.stack(
        [
            lax.ppermute(residual, ALL, moves(lambda tt, x, z, h: (x, tt, z, h))),
            lax.ppermute(residual, ALL, moves(lambda tt, x, z, h: (x, tt, z, 1 - h))),
        ]
    )
    shard = lax.ppermute(panels, ALL, moves(lambda tt, x, z, h: (z % 2 * 2 + h, tt, x, z // 2)))
    both, held, shard = lax.optimization_barrier((both, held, shard))
    held = spread(held, steps[1])
    left = toks - FIRST_PART
    part_a = jnp.concatenate(ring(both[:, :FIRST_PART], False))
    part_d = jnp.concatenate(ring(both[:, FIRST_PART:], True))
    held = spread(spread(held, steps[2]), steps[3])
    part_a, part_d, first_panel, shard, residual, weight = lax.optimization_barrier(
        (part_a, part_d, held, shard, residual, weight)
    )
    part_a = ring(part_a, True)
    part_d = ring(part_d, False)

    packed, part_a, part_d, first_panel, shard, residual = lax.optimization_barrier(
        (pack(weight, feats), part_a, part_d, first_panel, shard, residual)
    )
    moved = lax.all_to_all(packed, "tp", split_axis=0, concat_axis=0)
    pad = -(-rows // 128) * 128 - rows
    codes = jnp.pad(scale_codes.astype(jnp.float32).T, ((0, 0), (0, pad)))
    zeros = jnp.pad(zero_points.astype(jnp.float32).T, ((0, 0), (0, pad)))
    errors = block_errors(weight[:, :COLS], codes, zeros, first_panel)

    pair = beside(jnp.concatenate([residual, shard], axis=1))
    met = beyond(pair)
    own = met[:, :, :feats]
    own_panel = jnp.concatenate(
        [lax.dynamic_index_in_dim(met, t ^ i, 0, keepdims=False)[:, feats:] for i in range(groups)], axis=1
    )
    part_a = jnp.stack(part_a).reshape(4, 4, 2, FIRST_PART, feats)
    part_d = jnp.stack(part_d).reshape(4, 4, 2, left, feats)

    sums = jnp.concatenate(
        [
            jnp.sum(jnp.square(part_a.astype(jnp.float32)), axis=(1, 2, 4)),
            jnp.sum(jnp.square(part_d.astype(jnp.float32)), axis=(0, 2, 4)),
        ],
        axis=1,
    )
    sums = sums + lax.ppermute(sums, ALL, moves(lambda tt, x, z, h: (tt ^ 1, x, z, h)))
    sums = sums + lax.ppermute(sums, ALL, moves(lambda tt, x, z, h: (tt ^ 2, x, z, h)))
    copies = later(jnp.broadcast_to(errors[None], (shards, rows, COLS)), moved, met, sums)
    errors_all = lax.all_to_all(copies, "tp", split_axis=0, concat_axis=0)
    inv_norm = lax.rsqrt(sums / feat_total + EPS)[:, :, None]
    quarter_feats = feat_total // groups
    gain_rows = lax.dynamic_slice_in_dim(norm_gain, t * quarter_feats, quarter_feats, 0)
    gain_own = lax.dynamic_slice_in_dim(norm_gain, p * feats, feats, 0)
    table = jnp.stack(
        [((x + d) % 4) ^ t for d in RING]
        + [((z + d) % 4) * 2 + (h ^ c) for d in RING for c in range(2)]
    ).astype(jnp.int32)
    gram = mean_outer(part_a, part_d, own, inv_norm, gain_rows, gain_own, table)

    return (gram, corrected(moved, errors_all, own_panel))


def solution(mesh):
    in_specs = (
        P("tok", "tp"),
        P(),
        P(("tok", "tp"), None),
        P(("tok", "tp"), None),
        P(("tok", "tp"), None),
        P(None, ("tok", "tp")),
    )
    out_specs = (P("tok", "tp"), P("tok", "tp"))
    return jax.shard_map(
        on_device, mesh=mesh, in_specs=in_specs, out_specs=out_specs, check_vma=False
    )
```

```python
import functools
import math

import jax
import jax.numpy as jnp
from jax import lax
from jax.experimental import pallas as pl
from jax.experimental.pallas import tpu as pltpu
from jax.sharding import PartitionSpec as P

BLOCK = 128
BLOCKS = 2
COLS = BLOCK * BLOCKS
SUB = 8

EPS = 1e-05
SOFTNESS = 0.9
ALL = ("tok", "tp")

SINE = tuple(
    c * SOFTNESS / (2.0 * math.pi)
    for c in (
        6.283182818496983,
        -41.341421393740156,
        81.59618374823393,
        -76.58009925759313,
        41.20538928368347,
        -12.271253496065944,
    )
)


def tp_index(x, z, h):
    return x * 8 + z * 2 + h


def index(t, x, z, h):
    return t * 32 + tp_index(x, z, h)


PLACES = [(t, x, z, h) for t in range(4) for x in range(4) for z in range(4) for h in range(2)]


def moves(fn):
    return [(index(*a), index(*fn(*a))) for a in PLACES]


def split3(v):
    hi = v.astype(jnp.bfloat16).astype(jnp.float32)
    rest = v - hi
    mid = rest.astype(jnp.bfloat16).astype(jnp.float32)
    return hi, mid, rest - mid


def contract_rows(a, b):
    return lax.dot_general(a, b, (((0,), (0,)), ((), ())), preferred_element_type=jnp.float32)


def errors_kernel(w_ref, codes_ref, zeros_ref, p_ref, e_ref, work, diag, panel, errs):
    rows = w_ref.shape[0]
    lanes = work.shape[1]
    w = w_ref[...].astype(jnp.float32)
    w = jnp.concatenate([w, jnp.zeros((lanes - rows, COLS), jnp.float32)], axis=0)
    work[...] = w.T
    panel[...] = p_ref[...].astype(jnp.float32)
    across = panel[...].T
    row_id = lax.broadcasted_iota(jnp.int32, (COLS, COLS), 0)
    col_id = lax.broadcasted_iota(jnp.int32, (COLS, COLS), 1)
    pivots = jnp.sum(jnp.where(row_id == col_id, across, 0.0), axis=1, keepdims=True)
    diag[:, SUB : SUB + 1] = 1.0 / pivots
    for g in range(COLS // SUB):
        diag[g * SUB : (g + 1) * SUB, :SUB] = across[g * SUB : (g + 1) * SUB, g * SUB : (g + 1) * SUB]
    sub_id = lax.broadcasted_iota(jnp.int32, (SUB, lanes), 0)
    for k in range(BLOCKS):
        first = k * BLOCK
        half = codes_ref[k : k + 1, :] * 0.5 - 3.0
        scale = jnp.broadcast_to(jnp.exp2(half), (SUB, lanes))
        inverse = jnp.broadcast_to(jnp.exp2(-half), (SUB, lanes))
        zero = jnp.broadcast_to(zeros_ref[k : k + 1, :], (SUB, lanes))

        def group(g, carry):
            base = pl.multiple_of(first + g * SUB, SUB)
            now = work[pl.ds(base, SUB), :]
            local = diag[pl.ds(base, SUB), :]
            inv_pivot = jnp.broadcast_to(local[:, SUB : SUB + 1], (SUB, lanes))
            found = jnp.zeros((SUB, lanes), jnp.float32)
            for i in range(SUB):
                u = now * inverse + zero
                r = u - jnp.round(u)
                r2 = r * r
                r4 = r2 * r2
                wave = (SINE[0] + SINE[1] * r2) + r4 * (
                    (SINE[2] + SINE[3] * r2) + r4 * (SINE[4] + SINE[5] * r2)
                )
                soft = jnp.clip(u - wave * r, 0.0, 15.0)
                error = (now - scale * (soft - zero)) * inv_pivot
                error = jnp.broadcast_to(error[i : i + 1, :], (SUB, lanes))
                now = now - jnp.broadcast_to(local[:, i : i + 1], (SUB, lanes)) * error
                found = jnp.where(sub_id == i, error, found)
            errs[pl.ds(base, SUB), :] = found
            p_rows = panel[pl.ds(base, SUB), first : first + BLOCK]
            p_rows = jnp.concatenate([p_rows] * 3, axis=0).astype(jnp.bfloat16)
            e_rows = jnp.concatenate(split3(found), axis=0).astype(jnp.bfloat16)
            work[first : first + BLOCK, :] -= contract_rows(p_rows, e_rows)
            return carry

        lax.fori_loop(0, BLOCK // SUB, group, 0)
        if k + 1 < BLOCKS:
            p_rows = panel[first : first + BLOCK, first + BLOCK :].astype(jnp.bfloat16)
            spill = 0.0
            for part in split3(errs[first : first + BLOCK, :]):
                spill = spill + contract_rows(p_rows, part.astype(jnp.bfloat16))
            work[first + BLOCK :, :] -= spill
    found = errs[...].T[:rows].astype(jnp.bfloat16)
    for i in range(e_ref.shape[0]):
        e_ref[i] = found


def block_errors(weight, codes, zeros, first_panel, shards):
    rows = weight.shape[0]
    lanes = -(-rows // 128) * 128
    return pl.pallas_call(
        errors_kernel,
        grid=(1,),
        out_shape=jax.ShapeDtypeStruct((shards, rows, COLS), jnp.bfloat16),
        in_specs=[
            pl.BlockSpec((rows, COLS), lambda i: (0, 0)),
            pl.BlockSpec((BLOCKS, lanes), lambda i: (0, 0)),
            pl.BlockSpec((BLOCKS, lanes), lambda i: (0, 0)),
            pl.BlockSpec((COLS, COLS), lambda i: (0, 0)),
        ],
        out_specs=pl.BlockSpec((shards, rows, COLS), lambda i: (0, 0, 0)),
        scratch_shapes=[
            pltpu.VMEM((COLS, lanes), jnp.float32),
            pltpu.VMEM((COLS, 128), jnp.float32),
            pltpu.VMEM((COLS, COLS), jnp.float32),
            pltpu.VMEM((COLS, lanes), jnp.float32),
        ],
        compiler_params=pltpu.CompilerParams(vmem_limit_bytes=24 * 2**20),
        cost_estimate=pl.CostEstimate(flops=10**7, bytes_accessed=10**6, transcendentals=0),
        name="errors",
    )(weight, codes, zeros, first_panel)


RING = (0, 1, -1, 2)
FIRST_PART = 128


def gram_kernel(total, table, a_ref, d_ref, own_ref, inv_ref, gain_rows_ref, gain_own_ref, out_ref, own):
    groups, toks = own_ref.shape[:2]

    @pl.when(pl.program_id(0) == 0)
    def _():
        for g in range(groups):
            v = own_ref[table[g]].astype(jnp.float32) * inv_ref[g] * gain_own_ref[...]
            own[g * toks : (g + 1) * toks] = v.astype(jnp.bfloat16)

    parts = []
    for g in range(groups):
        v = jnp.concatenate([a_ref[g, 0, 0], d_ref[0, g, 0]], axis=0).astype(jnp.float32)
        parts.append((v * inv_ref[g] * gain_rows_ref[0]).astype(jnp.bfloat16))
    out_ref[...] = contract_rows(jnp.concatenate(parts, axis=0), own[...]) * (1.0 / total)


def mean_outer(part_a, part_d, own, inv_norm, gain_rows, gain_own, table):
    groups, toks, feats = own.shape
    pieces = 2 * groups
    spec = pltpu.PrefetchScalarGridSpec(
        num_scalar_prefetch=1,
        grid=(pieces,),
        in_specs=[
            pl.BlockSpec((groups, 1, 1) + part_a.shape[3:], lambda i, s: (0, i // 2, i % 2, 0, 0)),
            pl.BlockSpec((1, groups, 1) + part_d.shape[3:], lambda i, s: (i // 2, 0, i % 2, 0, 0)),
            pl.BlockSpec((groups, toks, feats), lambda i, s: (0, 0, 0)),
            pl.BlockSpec((groups, toks, 1), lambda i, s: (0, 0, 0)),
            pl.BlockSpec((1, 1, feats), lambda i, s: (s[groups + i], 0, 0)),
            pl.BlockSpec((1, feats), lambda i, s: (0, 0)),
        ],
        out_specs=pl.BlockSpec((feats, feats), lambda i, s: (s[groups + i], 0)),
        scratch_shapes=[pltpu.VMEM((groups * toks, feats), jnp.bfloat16)],
    )
    return pl.pallas_call(
        functools.partial(gram_kernel, groups * toks),
        grid_spec=spec,
        out_shape=jax.ShapeDtypeStruct((pieces * feats, feats), jnp.float32),
        compiler_params=pltpu.CompilerParams(vmem_limit_bytes=32 * 2**20),
        cost_estimate=pl.CostEstimate(
            flops=2 * groups * toks * pieces * feats * feats,
            bytes_accessed=20 * 2**20,
            transcendentals=0,
        ),
        name="mean_outer",
    )(table, part_a, part_d, own, inv_norm, gain_rows.reshape(pieces, 1, feats), gain_own.reshape(1, feats))


def corrected_kernel(w_ref, e_ref, p_ref, out_ref):
    rows, feats = out_ref.shape
    correction = jnp.dot(e_ref[...].reshape(rows, COLS), p_ref[...], preferred_element_type=jnp.float32)
    value = w_ref[...].reshape(rows, feats).astype(jnp.float32) - correction
    out_ref[...] = value.astype(jnp.bfloat16)


def corrected(moved, errors, panel):
    shards, rows, feats = moved.shape
    step = 4
    return pl.pallas_call(
        corrected_kernel,
        grid=(shards // step,),
        out_shape=jax.ShapeDtypeStruct((shards * rows, feats), jnp.bfloat16),
        in_specs=[
            pl.BlockSpec((step, rows, feats), lambda i: (i, 0, 0)),
            pl.BlockSpec((step, rows, COLS), lambda i: (i, 0, 0)),
            pl.BlockSpec((COLS, feats), lambda i: (0, 0)),
        ],
        out_specs=pl.BlockSpec((step * rows, feats), lambda i: (i, 0)),
        compiler_params=pltpu.CompilerParams(vmem_limit_bytes=32 * 2**20),
        cost_estimate=pl.CostEstimate(
            flops=2 * shards * rows * feats * COLS, bytes_accessed=20 * 2**20, transcendentals=0
        ),
        name="corrected",
    )(moved, errors, panel)


def pack_kernel(w_ref, out_ref):
    feats = out_ref.shape[2]
    for i in range(out_ref.shape[0]):
        out_ref[i] = w_ref[:, i * feats : (i + 1) * feats]


def pack(weight, feats):
    rows, total = weight.shape
    shards = total // feats
    return pl.pallas_call(
        pack_kernel,
        grid=(shards // 2,),
        out_shape=jax.ShapeDtypeStruct((shards, rows, feats), weight.dtype),
        in_specs=[pl.BlockSpec((rows, 2 * feats), lambda i: (0, i))],
        out_specs=pl.BlockSpec((2, rows, feats), lambda i: (i, 0, 0)),
        cost_estimate=pl.CostEstimate(flops=0, bytes_accessed=4 * rows * total, transcendentals=0),
        name="pack",
    )(weight)


def shift(d, along_x):
    if along_x:
        return moves(lambda t, x, z, h: (t, (x + d) % 4, z, h))
    return moves(lambda t, x, z, h: (t, x, (z + d) % 4, h))


def ring(block, along_x):
    others = [lax.ppermute(block, ALL, shift(-d, along_x)) for d in RING[1:]]
    return [block] + others


def beside(block):
    return jnp.stack([block, lax.ppermute(block, ALL, moves(lambda t, x, z, h: (t ^ 1, x, z, h)))])


def beyond(pair):
    return jnp.concatenate([pair, lax.ppermute(pair, ALL, moves(lambda t, x, z, h: (t ^ 2, x, z, h)))])


def later(value, *others):
    return lax.optimization_barrier((value,) + others)[0]


def first_columns(panels, t, p):
    nothing = jnp.zeros_like(panels)
    held = jnp.concatenate(
        [
            jnp.where((t == 0) & (p == 0), panels, nothing),
            jnp.where((t == 0) & (p == 1), panels, nothing),
        ],
        axis=1,
    )
    four, two = range(4), range(2)
    steps = [
        [[(index(0, 0, 0, h), index(0, 0, 0, 1 - h)) for h in two]],
        [[(index(0, 0, 0, h), index(0, x, 0, h)) for h in two] for x in (1, 2, 3)],
        [[(index(0, x, 0, h), index(0, x, z, h)) for x in four for h in two] for z in (1, 2, 3)],
        [
            [(index(0, x, z, h), index(t, x, z, h)) for x in four for z in four for h in two]
            for t in (1, 2, 3)
        ],
    ]
    return held, steps


def spread(held, perms):
    for got in [lax.ppermute(held, ALL, perm) for perm in perms]:
        held = held + got
    return held


def on_device(residual, norm_gain, weight, scale_codes, zero_points, panels):
    toks, feats = residual.shape
    rows, feat_total = weight.shape
    t = lax.axis_index("tok")
    p = lax.axis_index("tp")
    x, z, h = p // 8, p // 2 % 4, p % 2
    shards = lax.axis_size("tp")
    groups = lax.axis_size("tok")

    held, steps = first_columns(panels, t, p)
    held = spread(held, steps[0])
    both = jnp.stack(
        [
            lax.ppermute(residual, ALL, moves(lambda tt, x, z, h: (x, tt, z, h))),
            lax.ppermute(residual, ALL, moves(lambda tt, x, z, h: (x, tt, z, 1 - h))),
        ]
    )
    shard = lax.ppermute(panels, ALL, moves(lambda tt, x, z, h: (z % 2 * 2 + h, tt, x, z // 2)))
    both, held, shard = lax.optimization_barrier((both, held, shard))
    held = spread(held, steps[1])
    left = toks - FIRST_PART
    part_a = jnp.concatenate(ring(both[:, :FIRST_PART], False))
    part_d = jnp.concatenate(ring(both[:, FIRST_PART:], True))
    held = spread(spread(held, steps[2]), steps[3])
    part_a, part_d, first_panel, shard, residual, weight = lax.optimization_barrier(
        (part_a, part_d, held, shard, residual, weight)
    )
    part_a = ring(part_a, True)
    part_d = ring(part_d, False)

    packed, part_a, part_d, first_panel, shard, residual = lax.optimization_barrier(
        (pack(weight, feats), part_a, part_d, first_panel, shard, residual)
    )
    moved = lax.all_to_all(packed, "tp", split_axis=0, concat_axis=0)
    pad = -(-rows // 128) * 128 - rows
    codes = jnp.pad(scale_codes.astype(jnp.float32).T, ((0, 0), (0, pad)))
    zeros = jnp.pad(zero_points.astype(jnp.float32).T, ((0, 0), (0, pad)))
    errors = block_errors(weight[:, :COLS], codes, zeros, first_panel, shards)

    pair = beside(jnp.concatenate([residual, shard], axis=1))
    met = beyond(pair)
    own = met[:, :, :feats]
    own_panel = jnp.concatenate(
        [lax.dynamic_index_in_dim(met, t ^ i, 0, keepdims=False)[:, feats:] for i in range(groups)], axis=1
    )
    part_a = jnp.stack(part_a).reshape(4, 4, 2, FIRST_PART, feats)
    part_d = jnp.stack(part_d).reshape(4, 4, 2, left, feats)

    sums = jnp.concatenate(
        [
            jnp.sum(jnp.square(part_a.astype(jnp.float32)), axis=(1, 2, 4)),
            jnp.sum(jnp.square(part_d.astype(jnp.float32)), axis=(0, 2, 4)),
        ],
        axis=1,
    )
    sums = sums + lax.ppermute(sums, ALL, moves(lambda tt, x, z, h: (tt ^ 1, x, z, h)))
    sums = sums + lax.ppermute(sums, ALL, moves(lambda tt, x, z, h: (tt ^ 2, x, z, h)))
    copies = later(errors, moved, met, sums)
    errors_all = lax.all_to_all(copies, "tp", split_axis=0, concat_axis=0)
    inv_norm = lax.rsqrt(sums / feat_total + EPS)[:, :, None]
    quarter_feats = feat_total // groups
    gain_rows = lax.dynamic_slice_in_dim(norm_gain, t * quarter_feats, quarter_feats, 0)
    gain_own = lax.dynamic_slice_in_dim(norm_gain, p * feats, feats, 0)
    table = jnp.stack(
        [((x + d) % 4) ^ t for d in RING]
        + [((z + d) % 4) * 2 + (h ^ c) for d in RING for c in range(2)]
    ).astype(jnp.int32)
    gram = mean_outer(part_a, part_d, own, inv_norm, gain_rows, gain_own, table)

    return (gram, corrected(moved, errors_all, own_panel))


def solution(mesh):
    in_specs = (
        P("tok", "tp"),
        P(),
        P(("tok", "tp"), None),
        P(("tok", "tp"), None),
        P(("tok", "tp"), None),
        P(None, ("tok", "tp")),
    )
    out_specs = (P("tok", "tp"), P("tok", "tp"))
    return jax.shard_map(
        on_device, mesh=mesh, in_specs=in_specs, out_specs=out_specs, check_vma=False
    )
```
